256 devices in a mesh: wave: 64 (over x, z, core), lev: 4 (over y).
Axes of the slice: x: 4, y: 4, z: 8, core: 2. Of those that a mesh axis runs over, the one named last changes fastest.
Arguments:
- spectral: float32 [64, 128, 2, 1280], P('wave', 'lev'), may hold values from -6 to 6
- legendre: bfloat16 [64, 1280, 1280], P('wave'), may hold values from -0.15625 to 0.15625
- gauss_weight: float32 [1280], replicated, may hold values from 0.5 to 2
- slot_waves: int32 [64], replicated, may hold values from 0 to 63, each once
- grid_factor: float32 [2560, 4096], P('wave'), may hold values from -6 to 6
- mode_projector: float32 [128, 128], replicated, may hold values from -1 to 2
- vertical_modes: float32 [128, 128], replicated, may hold values from -1 to 2
- mode_rates: float32 [128], replicated, may hold values from 0.05 to 5
Outputs:
- advanced: float32 [64, 128, 2, 1280], P('wave', 'lev')
The draws below stay inside these ranges and needn't reach their ends.
Inputs may be any that keep to these rules, and one draw needn't show every extreme that they name: slot_waves holds every number of 0 to 63 once.
All inputs are finite; a program needn't handle non-finite values.
Results may differ from the reference program's by a relative error of at most 0.0051.
Values may be sent and summed in bfloat16 or wider, within the bound.
A program may use at most 64 MiB of HBM per device.

```python
import math
import jax
import jax.numpy as jnp
from jax import lax

NTR = 1280
NHALF = 1280
NLON = 4096
LEV = 128
M = 64
STRIDE = 19
NLAT = 2560


def draw_mode_projector(key, part):
    key = jax.random.fold_in(key, 7)
    noise = jax.random.normal(key, (LEV, LEV), jnp.float32)
    return jnp.eye(LEV, dtype=jnp.float32) + noise * (0.6 / math.sqrt(LEV))


def draw_vertical_modes(key, part):
    key = jax.random.fold_in(key, 13)
    noise = jax.random.normal(key, (LEV, LEV), jnp.float32)
    return jnp.eye(LEV, dtype=jnp.float32) + noise * (0.6 / math.sqrt(LEV))


def shard_levels(stream_key, shape, split, smallest, top_value):
    factor_of = 1.0
    for dim, shards_of in split:
        heights = jax.random.uniform(jax.random.fold_in(jax.random.fold_in(stream_key, 6), dim), (shards_of,), jnp.float32, smallest / len(split), top_value / len(split))
        factor_of = factor_of * jnp.repeat(jnp.exp(heights), shape[dim] // shards_of).reshape((-1,) + (1,) * (len(shape) - 1 - dim))
    return factor_of


def centred(key, shape, scale, most, cuts=(), kind=jnp.bfloat16):
    gain = shard_levels(key, shape, cuts, -0.22, 0.18) if cuts else 1.0
    values = jax.random.normal(key, shape, jnp.float32) * scale * gain
    return jnp.minimum(jnp.maximum(values, -most), most).astype(kind)


def setup_inputs(seed: int = 0) -> dict:
    arg_keys = jax.random.split(jax.random.key(seed), 9)
    spectral = centred(arg_keys[0], (M, LEV, 2, NTR), 1.0, 6.0, ((0, 64), (1, 4)), jnp.float32)
    legendre = centred(arg_keys[1], (M, NHALF, NTR), NTR ** -0.5, 0.15625, ((0, 64),))
    gauss_weight = jnp.clip(jnp.exp(jax.random.uniform(arg_keys[2], (NHALF,), jnp.float32, math.log(0.5), math.log(2.0))), 0.5, 2.0)
    slot_waves = jax.random.permutation(arg_keys[3], M).astype(jnp.int32)
    grid_factor = centred(arg_keys[4], (NLAT, NLON), 1.0, 6.0, ((0, 64),), jnp.float32)
    mode_projector = draw_mode_projector(jax.random.fold_in(arg_keys[8], 71), 0)
    vertical_modes = draw_vertical_modes(jax.random.fold_in(arg_keys[8], 71), 0)
    mode_rates = jnp.clip(jnp.exp(jax.random.uniform(arg_keys[7], (LEV,), jnp.float32, math.log(0.05), math.log(5.0))), 0.05, 5.0)
    return {"spectral": spectral, "legendre": legendre, "gauss_weight": gauss_weight, "slot_waves": slot_waves, "grid_factor": grid_factor, "mode_projector": mode_projector, "vertical_modes": vertical_modes, "mode_rates": mode_rates}


time_step = 0.5
square_weight = 0.3

def reference(spectral, legendre, gauss_weight, slot_waves, grid_factor, mode_projector, vertical_modes, mode_rates):
    waves = slot_waves * STRIDE
    order_index = jnp.arange(NTR, dtype=jnp.int32)
    live = (order_index[None, :] < (NTR - waves)[:, None]).astype(jnp.float32)
    parity = jnp.where(order_index % 2 == 0, 1.0, -1.0).astype(jnp.float32)
    masked = spectral * live[:, None, None, :]
    width = 2 * LEV
    coeffs = masked.reshape(M, width, NTR).astype(jnp.bfloat16)

    def inverse_one(args):
        table_rows, rows = args
        stacked = jnp.concatenate([rows, rows * parity.astype(jnp.bfloat16)], axis=0)
        fields = jnp.dot(table_rows, stacked.T, preferred_element_type=jnp.float32)
        return jnp.concatenate([fields[:, :width], fields[::-1, width:]], axis=0).astype(jnp.bfloat16)
    fourier = lax.map(inverse_one, (legendre, coeffs)).reshape(M, NLAT, LEV, 2)
    longitude = jnp.arange(NLON, dtype=jnp.int32)
    phase = waves[:, None] * longitude[None, :] % NLON
    angle = phase.astype(jnp.float32) * (2.0 * math.pi / NLON)
    table = jnp.stack([jnp.cos(angle), -jnp.sin(angle)], axis=1).astype(jnp.bfloat16)
    wide_table = table.astype(jnp.float32)
    block = math.gcd(NLAT, 8)
    count = NLAT // block
    blocks = fourier.reshape(M, count, block, LEV, 2).transpose(1, 0, 2, 3, 4)
    factors = grid_factor.reshape(count, block, NLON)

    def one_block(args):
        piece, factor = args
        grid = jnp.einsum('sbvr,srl->bvl', piece.astype(jnp.float32), wide_table) * (1.0 / math.sqrt(M))
        product = (factor[:, None, :] * grid + square_weight * grid * grid).astype(jnp.bfloat16)
        back = jnp.einsum('bvl,srl->sbvr', product.astype(jnp.float32), wide_table) * (1.0 / math.sqrt(NLON))
        return back.astype(jnp.bfloat16)
    backs = lax.map(one_block, (blocks, factors))
    backs = backs.transpose(1, 0, 2, 3, 4).reshape(M, NLAT, width)

    def direct_one(args):
        table_rows, rows = args
        both = jnp.concatenate([rows[:NHALF], rows[NHALF:][::-1]], axis=1).astype(jnp.float32)
        weighted = (both * gauss_weight[:, None]).astype(jnp.bfloat16)
        sums = jnp.dot(weighted.T, table_rows, preferred_element_type=jnp.float32)
        return sums[:width] + parity[None, :] * sums[width:]
    tendency = lax.map(direct_one, (legendre, backs)).reshape(M, LEV, 2, NTR) * live[:, None, None, :]
    rhs = masked + time_step * tendency
    degree = (waves[:, None] + order_index[None, :]).astype(jnp.float32)
    damping = degree * (degree + 1.0) / float(NTR * NTR)
    modes = jnp.einsum('jv,svrk->sjrk', mode_projector, rhs, precision=lax.Precision.HIGHEST)
    modes = modes / (1.0 + mode_rates[None, :, None, None] * damping[:, None, None, :])
    return jnp.einsum('vj,sjrk->svrk', vertical_modes, modes, precision=lax.Precision.HIGHEST)
```

```python
import functools
import math

import jax
import jax.numpy as jnp
import numpy as np
from jax import lax
from jax.experimental import pallas as pl
from jax.experimental.pallas import tpu as pltpu
from jax.sharding import PartitionSpec as P

time_step = 0.5
square_weight = 0.3
MESH = pl.DeviceIdType.MESH
f32, bf16 = jnp.float32, jnp.bfloat16
HIGHEST = lax.Precision.HIGHEST


@functools.lru_cache(maxsize=None)
def tables(slots, nlon, stride):
    points = 4 * slots
    step = nlon // points
    m = (np.arange(nlon, dtype=np.int64) * stride) % nlon
    i = np.arange(points, dtype=np.int64) * step
    q = np.arange(1, 2 * slots)
    series = 1.0 + 2.0 * np.cos(2.0 * np.pi * np.outer(np.arange(nlon), q) / nlon).sum(1)
    kernel = series[(m[None, :] - i[:, None]) % nlon] / nlon
    high = kernel.astype(np.float32).astype(jnp.bfloat16)
    low = (kernel - high.astype(np.float64)).astype(np.float32).astype(jnp.bfloat16)
    smooth = np.stack([part.T.reshape(nlon, -1, 128) for part in (high, low)], axis=1)
    smooth = np.ascontiguousarray(smooth.transpose(1, 2, 0, 3)).reshape(-1, nlon, 128)
    angle = 2.0 * np.pi * (np.outer(np.arange(points), np.arange(slots)) % points) / points
    waves = np.concatenate([np.cos(angle), -np.sin(angle)], axis=1)
    return smooth, waves.astype(np.float32).astype(jnp.bfloat16)


def dot(a, b, contract, precision=None):
    return lax.dot_general(
        a, b, (contract, ((), ())), precision=precision, preferred_element_type=f32
    )


def kernel(
    cfg,
    spec_h,
    leg_h,
    gw_h,
    sw_h,
    fac_h,
    mp_h,
    vm_h,
    mr_h,
    smooth_h,
    waves_h,
    out_ref,
    spec,
    leg,
    gw,
    sw,
    sw_s,
    fac,
    mp,
    vm,
    mr,
    smooth,
    waves,
    in_sem,
    leg_sem,
    own_sem,
    mask_out,
    mask_in,
    still_out,
    still_in,
    tend_out,
    tend_in,
    move_out,
    move_in,
    to_grid,
    at_grid,
    to_slot,
    at_slot,
    field,
    rows32,
    gwb,
    damp,
    fbig,
    trig,
    trig_t,
    lev_send,
    lev_recv,
    wave_send,
    wave_recv,
):
    slots, levs, half, orders, nlon, band, stride = cfg
    vl = spec.shape[0]
    lanes = 128
    groups = lanes // vl
    tiles = band // groups
    bands = half // band
    points = waves.shape[0]
    kq = orders // 2
    w = lax.axis_index("wave")
    y = lax.axis_index("lev")
    rows = 2 * tiles

    def load(src, dst, sem):
        cp = pltpu.make_async_copy(src, dst, sem)
        cp.start()
        return cp

    spec_cp = load(spec_h, spec, in_sem.at[0])
    sws_cp = load(sw_h, sw_s, in_sem.at[1])
    pieces = 5
    piece = half // pieces
    leg_cps = [
        load(leg_h.at[pl.ds(i * piece, piece)], leg.at[pl.ds(i * piece, piece)], leg_sem.at[i])
        for i in range(pieces)
    ]
    others = [
        load(a, b, in_sem.at[2 + i])
        for i, (a, b) in enumerate(
            [
                (sw_h, sw),
                (waves_h, waves),
                (gw_h, gw),
                (mr_h, mr),
                (mp_h, mp),
                (vm_h, vm),
                (fac_h, fac),
                (smooth_h, smooth),
            ]
        )
    ]

    barrier = pltpu.get_barrier_semaphore()

    def greet(i, _):
        pl.semaphore_signal(
            barrier, inc=1, device_id=(lax.rem(w + i, slots), y), device_id_type=MESH
        )
        return 0

    lax.fori_loop(1, slots, greet, 0)
    for i in range(1, levs):
        pl.semaphore_signal(
            barrier, inc=1, device_id=(w, lax.rem(y + i, levs)), device_id_type=MESH
        )

    sws_cp.wait()
    spec_cp.wait()
    wave = sw_s[w] * stride
    order = lax.broadcasted_iota(jnp.int32, (1, orders), 1)
    live = jnp.where(order < orders - wave, 1.0, 0.0).astype(f32)
    parity = jnp.where(order % 2 == 0, 1.0, -1.0).astype(f32)
    masked = [spec[:, r, :] * live for r in range(2)]
    for r in range(2):
        for h in range(2):
            mask_out[2 * r + h] = masked[r][:, h * kq : (h + 1) * kq]
    coeffs = jnp.concatenate(masked, axis=0)
    coeffs = jnp.concatenate([coeffs, coeffs * parity], axis=0).astype(bf16)
    for i in range(pieces):
        leg_cps[i].wait()
        field[pl.ds(i * piece, piece), :] = dot(
            leg[pl.ds(i * piece, piece), :], coeffs, ((1,), (1,))
        )

    lane = lax.broadcasted_iota(jnp.int32, (bands * tiles, lanes), 1) // vl

    def pick(parts, shift):
        acc = None
        for b in range(groups):
            turn = (shift(b) * vl) % lanes
            part = pltpu.roll(parts[b], turn, 1) if turn else parts[b]
            acc = part if acc is None else jnp.where(lane == b, part, acc)
        return acc

    block = bands * tiles
    cut = [field[pl.ds(a, block, stride=groups), :] for a in range(groups)]
    for n in range(2):
        for r in range(2):
            q = 2 * n + r
            rows32[pl.ds(n * 2 * block + r, block, stride=2), :] = pick(cut, lambda a: a - q)
    to_grid[...] = rows32[...].astype(bf16).reshape(to_grid.shape)

    pl.semaphore_wait(barrier, slots - 1 + levs - 1)

    def place(d):
        return d + (d // bands) * (3 * bands - 1 - 2 * d)

    def forward(i, _):
        d = lax.rem(w + i, slots)
        pltpu.make_async_remote_copy(
            src_ref=to_grid.at[place(d)],
            dst_ref=at_grid.at[w],
            send_sem=wave_send.at[0],
            recv_sem=wave_recv.at[0],
            device_id=(d, y),
            device_id_type=MESH,
        ).start()
        return 0

    lax.fori_loop(1, slots, forward, 0)
    own = pltpu.make_async_copy(to_grid.at[place(w)], at_grid.at[w], own_sem.at[0])
    own.start()

    def across(src, dst, k):
        cps = []
        for i in range(1, levs):
            to = lax.rem(y + i, levs)
            cp = pltpu.make_async_remote_copy(
                src_ref=src.at[to],
                dst_ref=dst.at[y],
                send_sem=lev_send.at[k, i - 1],
                recv_sem=lev_recv.at[k, i - 1],
                device_id=(w, to),
                device_id_type=MESH,
            )
            cp.start()
            cps.append(cp)
        dst[y] = src[y]
        return cps

    first = across(mask_out, mask_in, 0)

    for cp in others:
        cp.wait()
    for i in range(half // lanes):
        gwb[pl.ds(i * lanes, lanes), :] = jnp.broadcast_to(
            gw[pl.ds(i * lanes, lanes)].reshape(1, lanes), (lanes, lanes)
        ).T
    part_j = lax.broadcasted_iota(jnp.int32, (2 * slots, slots), 0)
    held = jnp.broadcast_to(sw[...].reshape(1, slots), (2 * slots, slots))
    choose = jnp.concatenate(
        [jnp.where(part_j == held + r * slots, 1.0, 0.0) for r in range(2)], axis=1
    ).astype(bf16)
    turned = dot(waves[...], choose, ((1,), (0,)))
    trig[...] = turned.astype(bf16)
    trig_t[...] = turned.T.astype(bf16)

    factor = fac[...]
    fhigh = factor.astype(bf16)
    flow = (factor - fhigh.astype(f32)).astype(bf16)
    half_points = points // lanes
    shigh, slow = [
        jnp.concatenate([smooth[n * half_points + i] for i in range(half_points)], axis=1)
        for n in range(2)
    ]
    top = dot(fhigh, shigh, ((1,), (0,))) + dot(flow, shigh, ((1,), (0,)))
    top += dot(fhigh, slow, ((1,), (0,)))
    root = 1.0 / math.sqrt(slots)
    top = top * root
    thigh = top.astype(bf16)
    tlow = (top - thigh.astype(f32)).astype(bf16)
    row = lax.broadcasted_iota(jnp.int32, (band, tiles * lanes), 0)
    south = w // bands
    row = row + south * (band - 1 - 2 * row)
    col = lax.broadcasted_iota(jnp.int32, (band, tiles * lanes), 1) // vl
    spread = jnp.where(row == col, 1.0, 0.0).astype(bf16)
    fbig[...] = dot(thigh, spread, ((0,), (0,))) + dot(tlow, spread, ((0,), (0,)))

    total = (wave + (y % 2) * kq + lax.broadcasted_iota(jnp.int32, (1, kq), 1)).astype(f32)
    damping = total * (total + 1.0) / float(orders * orders)
    rates = jnp.broadcast_to(mr[...].reshape(1, lanes), (lanes, lanes)).T[:, :1]
    damp[...] = 1.0 / (1.0 + rates * damping)

    def solve(x):
        modes = dot(mp[...], x, ((1,), (0,)), HIGHEST) * damp[...]
        return dot(vm[...], modes, ((1,), (0,)), HIGHEST)

    for cp in first:
        cp.wait()
    still_out[...] = solve(mask_in[...].reshape(levs * vl, kq)).reshape(levs, vl, kq)
    second = across(still_out, still_in, 1)

    own.wait()
    pltpu.make_async_copy(
        at_grid.at[pl.ds(0, slots - 1)], at_grid.at[pl.ds(0, slots - 1)], wave_recv.at[0]
    ).wait()
    rows32[...] = at_grid[...].reshape(slots * rows, lanes).astype(f32)
    for t in range(0, tiles, 2):
        piece_t = jnp.concatenate(
            [
                jnp.concatenate(
                    [rows32[pl.ds(2 * u + r, slots, stride=rows), :] for r in range(2)], axis=0
                )
                for u in (t, t + 1)
            ],
            axis=1,
        ).astype(bf16)
        grid = dot(trig[...], piece_t, ((1,), (0,)))
        fac_t = fbig[:, t * lanes : (t + 2) * lanes]
        product = (grid * (fac_t + (square_weight * root * root) * grid)).astype(bf16)
        back = dot(trig_t[...], product, ((1,), (0,)))
        back = back * ((nlon // points) / math.sqrt(nlon))
        for u in (t, t + 1):
            for r in range(2):
                field[pl.ds(2 * u + r, slots, stride=rows), :] = back[
                    r * slots : (r + 1) * slots, (u - t) * lanes : (u - t + 1) * lanes
                ]
    to_slot[...] = field[...].astype(bf16).reshape(to_slot.shape)

    def backward(i, _):
        d = lax.rem(w + i, slots)
        pltpu.make_async_remote_copy(
            src_ref=to_slot.at[d],
            dst_ref=at_slot.at[place(w)],
            send_sem=wave_send.at[1],
            recv_sem=wave_recv.at[1],
            device_id=(d, y),
            device_id_type=MESH,
        ).start()
        return 0

    lax.fori_loop(1, slots, backward, 0)
    own = pltpu.make_async_copy(to_slot.at[w], at_slot.at[place(w)], own_sem.at[1])
    own.start()
    own.wait()
    pltpu.make_async_copy(
        at_slot.at[pl.ds(0, slots - 1)], at_slot.at[pl.ds(0, slots - 1)], wave_recv.at[1]
    ).wait()

    rows32[...] = at_slot[...].reshape(slots * rows, lanes).astype(f32)
    cut = [
        rows32[pl.ds(n * 2 * block + r, block, stride=2), :] for n in range(2) for r in range(2)
    ]
    for a in range(groups):
        field[pl.ds(a, block, stride=groups), :] = pick(cut, lambda q: q - a)
    weighted = (field[...] * gwb[...]).astype(bf16)
    sums = dot(weighted, leg[...], ((0,), (0,)))
    tend = (sums[: 2 * vl] + parity * sums[2 * vl :]) * (live * time_step)
    for r in range(2):
        for h in range(2):
            tend_out[2 * r + h] = tend[r * vl : (r + 1) * vl, h * kq : (h + 1) * kq].astype(bf16)
    third = across(tend_out, tend_in, 2)
    for cp in third:
        cp.wait()
    change = tend_in[...].reshape(levs * vl, kq).astype(f32)
    move_out[...] = solve(change).reshape(levs, vl, kq).astype(bf16)
    fourth = across(move_out, move_in, 3)
    for cp in second:
        cp.wait()
    for cp in fourth:
        cp.wait()
    for r in range(2):
        for h in range(2):
            out_ref[:, r, h * kq : (h + 1) * kq] = still_in[2 * r + h] + move_in[
                2 * r + h
            ].astype(f32)
    for k, buf in ((0, to_grid), (1, to_slot)):
        pltpu.make_async_copy(
            buf.at[pl.ds(0, slots - 1)], buf.at[pl.ds(0, slots - 1)], wave_send.at[k]
        ).wait()


def local(
    spectral,
    legendre,
    gauss_weight,
    slot_waves,
    grid_factor,
    mode_projector,
    vertical_modes,
    mode_rates,
):
    _, vl, _, orders = spectral.shape
    half = legendre.shape[1]
    band, nlon = grid_factor.shape
    slots = slot_waves.shape[0]
    nmodes = mode_rates.shape[0]
    levs = nmodes // vl
    stride = ((orders - 1) // (slots - 1) - 1) // 2 * 2 + 1
    smooth, waves = tables(slots, nlon, stride)
    points = waves.shape[0]
    kq = orders // 2
    lanes = 128
    groups = lanes // vl
    tiles = band // groups
    cfg = (slots, levs, half, orders, nlon, band, stride)
    vmem = pltpu.VMEM
    dma = pltpu.SemaphoreType.DMA
    cells = vmem((slots, tiles, 2, lanes), bf16)
    scratch = [
        vmem((vl, 2, orders), f32),
        vmem((half, orders), bf16),
        vmem((half,), f32),
        vmem((slots,), jnp.int32),
        pltpu.SMEM((slots,), jnp.int32),
        vmem((band, nlon), f32),
        vmem((nmodes, nmodes), f32),
        vmem((nmodes, nmodes), f32),
        vmem((nmodes,), f32),
        vmem(smooth.shape, bf16),
        vmem(waves.shape, bf16),
        dma((10,)),
        dma((5,)),
        dma((2,)),
        vmem((levs, vl, kq), f32),
        vmem((levs, vl, kq), f32),
        vmem((levs, vl, kq), f32),
        vmem((levs, vl, kq), f32),
        vmem((levs, vl, kq), bf16),
        vmem((levs, vl, kq), bf16),
        vmem((levs, vl, kq), bf16),
        vmem((levs, vl, kq), bf16),
        cells,
        cells,
        cells,
        cells,
        vmem((half, lanes), f32),
        vmem((half, lanes), f32),
        vmem((half, lanes), f32),
        vmem((nmodes, kq), f32),
        vmem((points, tiles * lanes), f32),
        vmem((points, 2 * slots), bf16),
        vmem((2 * slots, points), bf16),
        dma((4, levs - 1)),
        dma((4, levs - 1)),
        dma((2,)),
        dma((2,)),
    ]
    out = pl.pallas_call(
        functools.partial(kernel, cfg),
        out_shape=jax.ShapeDtypeStruct((vl, 2, orders), f32),
        in_specs=[pl.BlockSpec(memory_space=pl.ANY)] * 10,
        out_specs=pl.BlockSpec(memory_space=vmem),
        scratch_shapes=scratch,
        compiler_params=pltpu.CompilerParams(
            collective_id=0, has_side_effects=True, vmem_limit_bytes=56 * 2**20
        ),
        name="round_trip",
    )(
        spectral[0],
        legendre[0],
        gauss_weight,
        slot_waves,
        grid_factor,
        mode_projector,
        vertical_modes,
        mode_rates,
        jnp.asarray(smooth),
        jnp.asarray(waves),
    )
    return out[None]


def solution(mesh):
    in_specs = (
        P("wave", "lev", None, None),
        P("wave", None, None),
        P(),
        P(),
        P("wave", None),
        P(),
        P(),
        P(),
    )
    out_specs = P("wave", "lev", None, None)
    return jax.shard_map(local, mesh=mesh, in_specs=in_specs, out_specs=out_specs, check_vma=False)
```

```python
import functools
import math

import jax
import jax.numpy as jnp
import numpy as np
from jax import lax
from jax.experimental import pallas as pl
from jax.experimental.pallas import tpu as pltpu
from jax.sharding import PartitionSpec as P

time_step = 0.5
square_weight = 0.3
MESH = pl.DeviceIdType.MESH
f32, bf16 = jnp.float32, jnp.bfloat16
HIGHEST = lax.Precision.HIGHEST


@functools.lru_cache(maxsize=None)
def tables(slots, nlon, stride):
    points = 4 * slots
    step = nlon // points
    m = (np.arange(nlon, dtype=np.int64) * stride) % nlon
    i = np.arange(points, dtype=np.int64) * step
    q = np.arange(1, 2 * slots)
    series = 1.0 + 2.0 * np.cos(2.0 * np.pi * np.outer(np.arange(nlon), q) / nlon).sum(1)
    kernel = series[(m[None, :] - i[:, None]) % nlon] / nlon
    high = kernel.astype(np.float32).astype(jnp.bfloat16)
    low = (kernel - high.astype(np.float64)).astype(np.float32).astype(jnp.bfloat16)
    smooth = np.stack([part.T.reshape(nlon, -1, 128) for part in (high, low)], axis=1)
    smooth = np.ascontiguousarray(smooth.transpose(1, 2, 0, 3)).reshape(-1, nlon, 128)
    angle = 2.0 * np.pi * (np.outer(np.arange(points), np.arange(slots)) % points) / points
    waves = np.concatenate([np.cos(angle), -np.sin(angle)], axis=1)
    return smooth, waves.astype(np.float32).astype(jnp.bfloat16)


def dot(a, b, contract, precision=None):
    return lax.dot_general(
        a, b, (contract, ((), ())), precision=precision, preferred_element_type=f32
    )


def kernel(
    cfg,
    spec_h,
    leg_h,
    gw_h,
    sw_h,
    fac_h,
    mp_h,
    vm_h,
    mr_h,
    smooth_h,
    waves_h,
    out_ref,
    spec,
    leg,
    gw,
    sw,
    sw_s,
    fac,
    mp,
    vm,
    mr,
    smooth,
    waves,
    in_sem,
    leg_sem,
    own_sem,
    mask_out,
    mask_in,
    still_out,
    still_in,
    tend_out,
    tend_in,
    move_out,
    move_in,
    to_grid,
    at_grid,
    to_slot,
    at_slot,
    field,
    rows32,
    gwb,
    damp,
    fbig,
    trig,
    trig_t,
    pair,
    lev_send,
    lev_recv,
    wave_send,
    wave_recv,
):
    slots, levs, half, orders, nlon, band, stride, cuts = cfg
    vl = spec.shape[0]
    lanes = 128
    groups = lanes // vl
    tiles = band // groups
    bands = half // band
    points = waves.shape[0]
    kq = orders // 2
    w = lax.axis_index("wave")
    y = lax.axis_index("lev")
    rows = 2 * tiles

    def load(src, dst, sem):
        cp = pltpu.make_async_copy(src, dst, sem)
        cp.start()
        return cp

    spec_cp = load(spec_h, spec, in_sem.at[0])
    sws_cp = load(sw_h, sw_s, in_sem.at[1])
    pieces = 5
    piece = half // pieces
    leg_cps = [
        load(leg_h.at[pl.ds(i * piece, piece)], leg.at[pl.ds(i * piece, piece)], leg_sem.at[i])
        for i in range(pieces)
    ]
    others = [
        load(a, b, in_sem.at[2 + i])
        for i, (a, b) in enumerate(
            [
                (sw_h, sw),
                (waves_h, waves),
                (gw_h, gw),
                (mr_h, mr),
                (mp_h, mp),
                (vm_h, vm),
                (fac_h, fac),
                (smooth_h, smooth),
            ]
        )
    ]

    barrier = pltpu.get_barrier_semaphore()

    def greet(i, _):
        pl.semaphore_signal(
            barrier, inc=1, device_id=(lax.rem(w + i, slots), y), device_id_type=MESH
        )
        return 0

    lax.fori_loop(1, slots, greet, 0)
    for i in range(1, levs):
        pl.semaphore_signal(
            barrier, inc=1, device_id=(w, lax.rem(y + i, levs)), device_id_type=MESH
        )

    sws_cp.wait()
    spec_cp.wait()
    wave = sw_s[w] * stride
    order = lax.broadcasted_iota(jnp.int32, (1, orders), 1)
    live = jnp.where(order < orders - wave, 1.0, 0.0).astype(f32)
    parity = jnp.where(order % 2 == 0, 1.0, -1.0).astype(f32)
    masked = [spec[:, r, :] * live for r in range(2)]
    for r in range(2):
        for h in range(2):
            mask_out[2 * r + h] = masked[r][:, h * kq : (h + 1) * kq]
    coeffs = jnp.concatenate(masked, axis=0)
    coeffs = jnp.concatenate([coeffs, coeffs * parity], axis=0).astype(bf16)
    for i in range(pieces):
        leg_cps[i].wait()
        field[pl.ds(i * piece, piece), :] = dot(
            leg[pl.ds(i * piece, piece), :], coeffs, ((1,), (1,))
        )

    lane = lax.broadcasted_iota(jnp.int32, (bands * tiles, lanes), 1) // vl

    def pick(parts, shift):
        acc = None
        for b in range(groups):
            turn = (shift(b) * vl) % lanes
            part = pltpu.roll(parts[b], turn, 1) if turn else parts[b]
            acc = part if acc is None else jnp.where(lane == b, part, acc)
        return acc

    block = bands * tiles
    cut = [field[pl.ds(a, block, stride=groups), :] for a in range(groups)]
    for n in range(2):
        for r in range(2):
            q = 2 * n + r
            rows32[pl.ds(n * 2 * block + r, block, stride=2), :] = pick(cut, lambda a: a - q)
    to_grid[...] = rows32[...].astype(bf16).reshape(to_grid.shape)

    pl.semaphore_wait(barrier, slots - 1 + levs - 1)

    def place(d):
        return d + (d // bands) * (3 * bands - 1 - 2 * d)

    def forward(c, i, _):
        d = lax.rem(w + i, slots)
        pltpu.make_async_remote_copy(
            src_ref=to_grid.at[place(d), pl.ds(*cuts[c])],
            dst_ref=at_grid.at[w, pl.ds(*cuts[c])],
            send_sem=wave_send.at[0, c],
            recv_sem=wave_recv.at[0, c],
            device_id=(d, y),
            device_id_type=MESH,
        ).start()
        return 0

    for c in range(len(cuts)):
        lax.fori_loop(1, slots, functools.partial(forward, c), 0)
    own = pltpu.make_async_copy(to_grid.at[place(w)], at_grid.at[w], own_sem.at[0])
    own.start()

    def across(src, dst, k):
        cps = []
        for i in range(1, levs):
            to = lax.rem(y + i, levs)
            cp = pltpu.make_async_remote_copy(
                src_ref=src.at[to],
                dst_ref=dst.at[y],
                send_sem=lev_send.at[k, i - 1],
                recv_sem=lev_recv.at[k, i - 1],
                device_id=(w, to),
                device_id_type=MESH,
            )
            cp.start()
            cps.append(cp)
        dst[y] = src[y]
        return cps

    first = across(mask_out, mask_in, 0)

    for cp in others:
        cp.wait()
    for i in range(half // lanes):
        gwb[pl.ds(i * lanes, lanes), :] = jnp.broadcast_to(
            gw[pl.ds(i * lanes, lanes)].reshape(1, lanes), (lanes, lanes)
        ).T
    part_j = lax.broadcasted_iota(jnp.int32, (2 * slots, slots), 0)
    held = jnp.broadcast_to(sw[...].reshape(1, slots), (2 * slots, slots))
    choose = jnp.concatenate(
        [jnp.where(part_j == held + r * slots, 1.0, 0.0) for r in range(2)], axis=1
    ).astype(bf16)
    turned = dot(waves[...], choose, ((1,), (0,)))
    trig[...] = turned.astype(bf16)
    trig_t[...] = turned.T.astype(bf16)

    factor = fac[...]
    fhigh = factor.astype(bf16)
    flow = (factor - fhigh.astype(f32)).astype(bf16)
    half_points = points // lanes
    shigh, slow = [
        jnp.concatenate([smooth[n * half_points + i] for i in range(half_points)], axis=1)
        for n in range(2)
    ]
    top = dot(fhigh, shigh, ((1,), (0,))) + dot(flow, shigh, ((1,), (0,)))
    top += dot(fhigh, slow, ((1,), (0,)))
    root = 1.0 / math.sqrt(slots)
    top = top * root
    thigh = top.astype(bf16)
    tlow = (top - thigh.astype(f32)).astype(bf16)
    row = lax.broadcasted_iota(jnp.int32, (band, tiles * lanes), 0)
    south = w // bands
    row = row + south * (band - 1 - 2 * row)
    col = lax.broadcasted_iota(jnp.int32, (band, tiles * lanes), 1) // vl
    spread = jnp.where(row == col, 1.0, 0.0).astype(bf16)
    fbig[...] = dot(thigh, spread, ((0,), (0,))) + dot(tlow, spread, ((0,), (0,)))

    total = (wave + (y % 2) * kq + lax.broadcasted_iota(jnp.int32, (1, kq), 1)).astype(f32)
    damping = total * (total + 1.0) / float(orders * orders)
    rates = jnp.broadcast_to(mr[...].reshape(1, lanes), (lanes, lanes)).T[:, :1]
    damp[...] = 1.0 / (1.0 + rates * damping)

    def solve(x):
        modes = dot(mp[...], x, ((1,), (0,)), HIGHEST) * damp[...]
        return dot(vm[...], modes, ((1,), (0,)), HIGHEST)

    def split(x):
        high = x.astype(bf16)
        return high, (x - high.astype(f32)).astype(bf16)

    ends = [split(ref[...]) for ref in (mp, vm)]
    for k in range(2):
        pair[k] = jnp.concatenate(ends[k], axis=1)

    def solve_change(x):
        modes = dot(pair[0], jnp.concatenate([x, x], axis=0), ((1,), (0,))) * damp[...]
        high, low = split(modes)
        out = dot(pair[1], jnp.concatenate([high, high], axis=0), ((1,), (0,)))
        return out + dot(pair[1, :, :lanes], low, ((1,), (0,)))

    for cp in first:
        cp.wait()
    still_out[...] = solve(mask_in[...].reshape(levs * vl, kq)).reshape(levs, vl, kq)
    second = across(still_out, still_in, 1)

    def await_all(buf, sems, c):
        ref = buf.at[pl.ds(0, slots - 1), pl.ds(*cuts[c])]
        pltpu.make_async_copy(ref, ref, sems.at[c]).wait()

    def backward(c, i, _):
        d = lax.rem(w + i, slots)
        pltpu.make_async_remote_copy(
            src_ref=to_slot.at[d, pl.ds(*cuts[c])],
            dst_ref=at_slot.at[place(w), pl.ds(*cuts[c])],
            send_sem=wave_send.at[1, c],
            recv_sem=wave_recv.at[1, c],
            device_id=(d, y),
            device_id_type=MESH,
        ).start()
        return 0

    own.wait()
    for c, (start, count) in enumerate(cuts):
        await_all(at_grid, wave_recv.at[0], c)
        chunk = 2 * count
        here = pl.ds(0, slots * chunk)
        rows32[here, :] = (
            at_grid[:, start : start + count].reshape(slots * chunk, lanes).astype(f32)
        )
        parts = jnp.concatenate(
            [
                jnp.concatenate(
                    [rows32[pl.ds(2 * u + r, slots, stride=chunk), :] for r in range(2)], axis=0
                ).astype(bf16)
                for u in range(count)
            ],
            axis=1,
        )
        grid = dot(trig[...], parts, ((1,), (0,)))
        scaled = fbig[:, start * lanes : (start + count) * lanes]
        product = (grid * (scaled + (square_weight * root * root) * grid)).astype(bf16)
        back = dot(trig_t[...], product, ((1,), (0,)))
        back = back * ((nlon // points) / math.sqrt(nlon))
        for u in range(count):
            for r in range(2):
                field[pl.ds(2 * u + r, slots, stride=chunk), :] = back[
                    r * slots : (r + 1) * slots, u * lanes : (u + 1) * lanes
                ]
        to_slot[:, start : start + count] = (
            field[here, :].astype(bf16).reshape(slots, count, 2, lanes)
        )
        lax.fori_loop(1, slots, functools.partial(backward, c), 0)
    own = pltpu.make_async_copy(to_slot.at[w], at_slot.at[place(w)], own_sem.at[1])
    own.start()
    own.wait()
    for c in range(len(cuts)):
        await_all(at_slot, wave_recv.at[1], c)

    rows32[...] = at_slot[...].reshape(slots * rows, lanes).astype(f32)
    cut = [
        rows32[pl.ds(n * 2 * block + r, block, stride=2), :] for n in range(2) for r in range(2)
    ]
    for a in range(groups):
        field[pl.ds(a, block, stride=groups), :] = pick(cut, lambda q: q - a)
    weighted = (field[...] * gwb[...]).astype(bf16)
    sums = dot(weighted, leg[...], ((0,), (0,)))
    tend = (sums[: 2 * vl] + parity * sums[2 * vl :]) * (live * time_step)
    for r in range(2):
        for h in range(2):
            tend_out[2 * r + h] = tend[r * vl : (r + 1) * vl, h * kq : (h + 1) * kq].astype(bf16)
    third = across(tend_out, tend_in, 2)
    for cp in third:
        cp.wait()
    change = tend_in[...].reshape(levs * vl, kq)
    move_out[...] = solve_change(change).reshape(levs, vl, kq).astype(bf16)
    fourth = across(move_out, move_in, 3)
    for cp in second:
        cp.wait()
    for cp in fourth:
        cp.wait()
    for r in range(2):
        for h in range(2):
            out_ref[:, r, h * kq : (h + 1) * kq] = still_in[2 * r + h] + move_in[
                2 * r + h
            ].astype(f32)
    for k, buf in ((0, to_grid), (1, to_slot)):
        for c in range(len(cuts)):
            await_all(buf, wave_send.at[k], c)


def local(
    spectral,
    legendre,
    gauss_weight,
    slot_waves,
    grid_factor,
    mode_projector,
    vertical_modes,
    mode_rates,
):
    _, vl, _, orders = spectral.shape
    half = legendre.shape[1]
    band, nlon = grid_factor.shape
    slots = slot_waves.shape[0]
    nmodes = mode_rates.shape[0]
    levs = nmodes // vl
    stride = ((orders - 1) // (slots - 1) - 1) // 2 * 2 + 1
    smooth, waves = tables(slots, nlon, stride)
    points = waves.shape[0]
    kq = orders // 2
    lanes = 128
    groups = lanes // vl
    tiles = band // groups
    first = tiles // 2
    cuts = ((0, first), (first, tiles - first))
    cfg = (slots, levs, half, orders, nlon, band, stride, cuts)
    vmem = pltpu.VMEM
    dma = pltpu.SemaphoreType.DMA
    cells = vmem((slots, tiles, 2, lanes), bf16)
    scratch = [
        vmem((vl, 2, orders), f32),
        vmem((half, orders), bf16),
        vmem((half,), f32),
        vmem((slots,), jnp.int32),
        pltpu.SMEM((slots,), jnp.int32),
        vmem((band, nlon), f32),
        vmem((nmodes, nmodes), f32),
        vmem((nmodes, nmodes), f32),
        vmem((nmodes,), f32),
        vmem(smooth.shape, bf16),
        vmem(waves.shape, bf16),
        dma((10,)),
        dma((5,)),
        dma((2,)),
        vmem((levs, vl, kq), f32),
        vmem((levs, vl, kq), f32),
        vmem((levs, vl, kq), f32),
        vmem((levs, vl, kq), f32),
        vmem((levs, vl, kq), bf16),
        vmem((levs, vl, kq), bf16),
        vmem((levs, vl, kq), bf16),
        vmem((levs, vl, kq), bf16),
        cells,
        cells,
        cells,
        cells,
        vmem((half, lanes), f32),
        vmem((half, lanes), f32),
        vmem((half, lanes), f32),
        vmem((nmodes, kq), f32),
        vmem((points, tiles * lanes), f32),
        vmem((points, 2 * slots), bf16),
        vmem((2 * slots, points), bf16),
        vmem((2, nmodes, 2 * nmodes), bf16),
        dma((4, levs - 1)),
        dma((4, levs - 1)),
        dma((2, len(cuts))),
        dma((2, len(cuts))),
    ]
    out = pl.pallas_call(
        functools.partial(kernel, cfg),
        out_shape=pltpu.VMEM((vl, 2, orders), f32),
        in_specs=[pl.BlockSpec(memory_space=pl.ANY)] * 10,
        out_specs=pl.BlockSpec(memory_space=vmem),
        scratch_shapes=scratch,
        compiler_params=pltpu.CompilerParams(
            collective_id=0, has_side_effects=True, vmem_limit_bytes=56 * 2**20
        ),
        name="round_trip",
    )(
        spectral[0],
        legendre[0],
        gauss_weight,
        slot_waves,
        grid_factor,
        mode_projector,
        vertical_modes,
        mode_rates,
        jnp.asarray(smooth),
        jnp.asarray(waves),
    )
    return out[None]


def solution(mesh):
    in_specs = (
        P("wave", "lev", None, None),
        P("wave", None, None),
        P(),
        P(),
        P("wave", None),
        P(),
        P(),
        P(),
    )
    out_specs = P("wave", "lev", None, None)
    return jax.shard_map(local, mesh=mesh, in_specs=in_specs, out_specs=out_specs, check_vma=False)
```

```python
import functools
import math

import jax
import jax.numpy as jnp
import numpy as np
from jax import lax
from jax.experimental import pallas as pl
from jax.experimental.pallas import tpu as pltpu
from jax.sharding import PartitionSpec as P

time_step = 0.5
square_weight = 0.3
MESH = pl.DeviceIdType.MESH
f32, bf16 = jnp.float32, jnp.bfloat16
HIGHEST = lax.Precision.HIGHEST


@functools.lru_cache(maxsize=None)
def tables(slots, nlon, stride):
    points = 4 * slots
    step = nlon // points
    m = (np.arange(nlon, dtype=np.int64) * stride) % nlon
    i = np.arange(points, dtype=np.int64) * step
    q = np.arange(1, 2 * slots)
    series = 1.0 + 2.0 * np.cos(2.0 * np.pi * np.outer(np.arange(nlon), q) / nlon).sum(1)
    kernel = series[(m[None, :] - i[:, None]) % nlon] / nlon
    high = kernel.astype(np.float32).astype(jnp.bfloat16)
    low = (kernel - high.astype(np.float64)).astype(np.float32).astype(jnp.bfloat16)
    smooth = np.stack([part.T.reshape(nlon, -1, 128) for part in (high, low)], axis=1)
    smooth = np.ascontiguousarray(smooth.transpose(1, 2, 0, 3)).reshape(-1, nlon, 128)
    angle = 2.0 * np.pi * (np.outer(np.arange(points), np.arange(slots)) % points) / points
    waves = np.concatenate([np.cos(angle), -np.sin(angle)], axis=1)
    return smooth, waves.astype(np.float32).astype(jnp.bfloat16)


@functools.lru_cache(maxsize=None)
def swap_blocks(groups, size):
    width = groups * groups * size
    at = np.arange(width).reshape(groups, groups, size).transpose(1, 0, 2).reshape(-1)
    swap = np.zeros((width, width), np.float32)
    swap[at, np.arange(width)] = 1.0
    swap = swap.reshape(width, -1, 128).transpose(1, 0, 2)
    return np.ascontiguousarray(swap).astype(jnp.bfloat16)


def dot(a, b, contract, precision=None):
    return lax.dot_general(
        a, b, (contract, ((), ())), precision=precision, preferred_element_type=f32
    )


def kernel(
    cfg,
    spec_h,
    leg_h,
    gw_h,
    sw_h,
    fac_h,
    mp_h,
    vm_h,
    mr_h,
    smooth_h,
    waves_h,
    swap_h,
    out_ref,
    spec,
    leg,
    gw,
    sw,
    sw_s,
    fac,
    mp,
    vm,
    mr,
    smooth,
    waves,
    swap,
    in_sem,
    leg_sem,
    own_sem,
    mask_out,
    mask_in,
    still_out,
    still_in,
    tend_out,
    tend_in,
    move_out,
    move_in,
    to_grid,
    at_grid,
    to_slot,
    at_slot,
    field,
    rows32,
    gwb,
    gwbc,
    legc,
    partial,
    damp,
    fbig,
    trig,
    trig_t,
    pair,
    lev_send,
    lev_recv,
    wave_send,
    wave_recv,
):
    slots, levs, half, orders, nlon, band, stride, cuts, splits = cfg
    vl = spec.shape[0]
    lanes = 128
    groups = lanes // vl
    tiles = band // groups
    bands = half // band
    points = waves.shape[0]
    kq = orders // 2
    w = lax.axis_index("wave")
    y = lax.axis_index("lev")
    rows = 2 * tiles

    barrier = pltpu.get_barrier_semaphore()

    def every_peer(act):
        def step(i, _):
            act(lax.rem(w + i, slots))
            return 0

        lax.fori_loop(1, slots, step, 0)

    def greet(d):
        pl.semaphore_signal(barrier, inc=1, device_id=(d, y), device_id_type=MESH)

    every_peer(greet)
    for i in range(1, levs):
        pl.semaphore_signal(
            barrier, inc=1, device_id=(w, lax.rem(y + i, levs)), device_id_type=MESH
        )

    def load(src, dst, sem):
        cp = pltpu.make_async_copy(src, dst, sem)
        cp.start()
        return cp

    spec_cp = load(spec_h, spec, in_sem.at[0])
    swap_cp = load(swap_h, swap, in_sem.at[10])
    sws_cp = load(sw_h, sw_s, in_sem.at[1])
    pieces = 5
    piece = half // pieces
    leg_cps = [
        load(leg_h.at[pl.ds(i * piece, piece)], leg.at[pl.ds(i * piece, piece)], leg_sem.at[i])
        for i in range(pieces)
    ]
    others = [
        load(a, b, in_sem.at[2 + i])
        for i, (a, b) in enumerate(
            [
                (sw_h, sw),
                (waves_h, waves),
                (gw_h, gw),
                (mr_h, mr),
                (mp_h, mp),
                (vm_h, vm),
                (fac_h, fac),
                (smooth_h, smooth),
            ]
        )
    ]

    sws_cp.wait()
    spec_cp.wait()
    wave = sw_s[w] * stride
    order = lax.broadcasted_iota(jnp.int32, (1, orders), 1)
    live = jnp.where(order < orders - wave, 1.0, 0.0).astype(f32)
    parity = jnp.where(order % 2 == 0, 1.0, -1.0).astype(f32)
    masked = [spec[:, r, :] * live for r in range(2)]
    for r in range(2):
        for h in range(2):
            mask_out[2 * r + h] = masked[r][:, h * kq : (h + 1) * kq]
    coeffs = jnp.concatenate(masked, axis=0)
    coeffs = jnp.concatenate([coeffs, coeffs * parity], axis=0).astype(bf16)
    for i in range(pieces):
        leg_cps[i].wait()
        field[pl.ds(i * piece, piece), :] = dot(
            leg[pl.ds(i * piece, piece), :], coeffs, ((1,), (1,))
        )

    block = bands * tiles
    swap_cp.wait()

    def swapped(parts):
        turn = jnp.concatenate([swap[i] for i in range(groups)], axis=1)
        return dot(jnp.concatenate(parts, axis=1), turn, ((1,), (0,)))

    turned = swapped(
        [field[pl.ds(a, block, stride=groups), :].astype(bf16) for a in range(groups)]
    )
    for n in range(2):
        for r in range(2):
            q = 2 * n + r
            rows32[pl.ds(n * 2 * block + r, block, stride=2), :] = turned[
                :, q * lanes : (q + 1) * lanes
            ]
    to_grid[...] = rows32[...].astype(bf16).reshape(to_grid.shape)

    pl.semaphore_wait(barrier, slots - 1 + levs - 1)

    def place(d):
        return d + (d // bands) * (3 * bands - 1 - 2 * d)

    def forward(c, d):
        pltpu.make_async_remote_copy(
            src_ref=to_grid.at[place(d), pl.ds(*cuts[c])],
            dst_ref=at_grid.at[w, pl.ds(*cuts[c])],
            send_sem=wave_send.at[0, c],
            recv_sem=wave_recv.at[0, c],
            device_id=(d, y),
            device_id_type=MESH,
        ).start()

    for c in range(len(cuts)):
        every_peer(functools.partial(forward, c))
    own = pltpu.make_async_copy(to_grid.at[place(w)], at_grid.at[w], own_sem.at[0])
    own.start()

    def across(src, dst, k):
        cps = []
        for i in (2, 1, 3):
            to = lax.rem(y + i, levs)
            cp = pltpu.make_async_remote_copy(
                src_ref=src.at[to],
                dst_ref=dst.at[y],
                send_sem=lev_send.at[k, i - 1],
                recv_sem=lev_recv.at[k, i - 1],
                device_id=(w, to),
                device_id_type=MESH,
            )
            cp.start()
            cps.append(cp)
        dst[y] = src[y]
        return cps

    first = across(mask_out, mask_in, 0)

    for cp in others:
        cp.wait()
    for i in range(half // lanes):
        gwb[pl.ds(i * lanes, lanes), :] = jnp.broadcast_to(
            gw[pl.ds(i * lanes, lanes)].reshape(1, lanes), (lanes, lanes)
        ).T
    base = 0
    for start, count in cuts:
        size = count * groups
        for i in range(bands):
            src, dst = pl.ds(i * band + start * groups, size), pl.ds(base + i * size, size)
            legc[dst, :] = leg[src, :]
            gwbc[dst, :] = gwb[src, :]
        base += bands * size
    part_j = lax.broadcasted_iota(jnp.int32, (2 * slots, slots), 0)
    held = jnp.broadcast_to(sw[...].reshape(1, slots), (2 * slots, slots))
    choose = jnp.concatenate(
        [jnp.where(part_j == held + r * slots, 1.0, 0.0) for r in range(2)], axis=1
    ).astype(bf16)
    turned = dot(waves[...], choose, ((1,), (0,)))
    trig[...] = turned.astype(bf16)
    trig_t[...] = turned.T.astype(bf16)

    factor = fac[...]
    fhigh = factor.astype(bf16)
    flow = (factor - fhigh.astype(f32)).astype(bf16)
    half_points = points // lanes
    shigh, slow = [
        jnp.concatenate([smooth[n * half_points + i] for i in range(half_points)], axis=1)
        for n in range(2)
    ]
    top = dot(fhigh, shigh, ((1,), (0,))) + dot(flow, shigh, ((1,), (0,)))
    top += dot(fhigh, slow, ((1,), (0,)))
    root = 1.0 / math.sqrt(slots)
    top = top * root
    thigh = top.astype(bf16)
    tlow = (top - thigh.astype(f32)).astype(bf16)
    row = lax.broadcasted_iota(jnp.int32, (band, tiles * lanes), 0)
    south = w // bands
    row = row + south * (band - 1 - 2 * row)
    col = lax.broadcasted_iota(jnp.int32, (band, tiles * lanes), 1) // vl
    spread = jnp.where(row == col, 1.0, 0.0).astype(bf16)
    fbig[...] = dot(thigh, spread, ((0,), (0,))) + dot(tlow, spread, ((0,), (0,)))

    total = (wave + (y % 2) * kq + lax.broadcasted_iota(jnp.int32, (1, kq), 1)).astype(f32)
    damping = total * (total + 1.0) / float(orders * orders)
    rates = jnp.broadcast_to(mr[...].reshape(1, lanes), (lanes, lanes)).T[:, :1]
    damp[...] = 1.0 / (1.0 + rates * damping)

    def solve(x):
        modes = dot(mp[...], x, ((1,), (0,)), HIGHEST) * damp[...]
        return dot(vm[...], modes, ((1,), (0,)), HIGHEST)

    def split(x):
        high = x.astype(bf16)
        return high, (x - high.astype(f32)).astype(bf16)

    ends = [split(ref[...]) for ref in (mp, vm)]
    for k in range(2):
        pair[k] = jnp.concatenate(ends[k], axis=1)

    def solve_change(x, damping):
        modes = dot(pair[0], jnp.concatenate([x, x], axis=0), ((1,), (0,))) * damping
        high, low = split(modes)
        out = dot(pair[1], jnp.concatenate([high, high], axis=0), ((1,), (0,)))
        return out + dot(pair[1, :, :lanes], low, ((1,), (0,)))

    for cp in first:
        cp.wait()
    still_out[...] = solve(mask_in[...].reshape(levs * vl, kq)).reshape(levs, vl, kq)
    second = across(still_out, still_in, 1)

    def await_all(buf, sems, c):
        ref = buf.at[pl.ds(0, slots - 1), pl.ds(*cuts[c])]
        pltpu.make_async_copy(ref, ref, sems.at[c]).wait()

    def backward(c, d):
        pltpu.make_async_remote_copy(
            src_ref=to_slot.at[d, pl.ds(*cuts[c])],
            dst_ref=at_slot.at[place(w), pl.ds(*cuts[c])],
            send_sem=wave_send.at[1, c],
            recv_sem=wave_recv.at[1, c],
            device_id=(d, y),
            device_id_type=MESH,
        ).start()

    own.wait()
    for c, (start, count) in enumerate(cuts):
        await_all(at_grid, wave_recv.at[0], c)
        chunk = 2 * count
        here = pl.ds(0, slots * chunk)
        rows32[here, :] = (
            at_grid[:, start : start + count].reshape(slots * chunk, lanes).astype(f32)
        )
        parts = jnp.concatenate(
            [
                jnp.concatenate(
                    [rows32[pl.ds(2 * u + r, slots, stride=chunk), :] for r in range(2)], axis=0
                ).astype(bf16)
                for u in range(count)
            ],
            axis=1,
        )
        grid = dot(trig[...], parts, ((1,), (0,)))
        scaled = fbig[:, start * lanes : (start + count) * lanes]
        product = (grid * (scaled + (square_weight * root * root) * grid)).astype(bf16)
        back = dot(trig_t[...], product, ((1,), (0,)))
        back = back * ((nlon // points) / math.sqrt(nlon))
        for u in range(count):
            for r in range(2):
                field[pl.ds(2 * u + r, slots, stride=chunk), :] = back[
                    r * slots : (r + 1) * slots, u * lanes : (u + 1) * lanes
                ]
        to_slot[:, start : start + count] = (
            field[here, :].astype(bf16).reshape(slots, count, 2, lanes)
        )
        every_peer(functools.partial(backward, c))
    own = pltpu.make_async_copy(to_slot.at[w], at_slot.at[place(w)], own_sem.at[1])
    own.start()
    own.wait()
    third = []
    base = 0
    for c, (start, count) in enumerate(cuts):
        await_all(at_slot, wave_recv.at[1], c)
        size = bands * count * groups
        some = bands * count
        rows32[pl.ds(0, slots * 2 * count), :] = (
            at_slot[:, start : start + count].reshape(slots * 2 * count, lanes).astype(f32)
        )
        turned = swapped(
            [
                rows32[pl.ds(n * 2 * some + r, some, stride=2), :].astype(bf16)
                for n in range(2)
                for r in range(2)
            ]
        )
        for a in range(groups):
            field[pl.ds(a, some, stride=groups), :] = turned[:, a * lanes : (a + 1) * lanes]
        weighted = (field[pl.ds(0, size), :] * gwbc[pl.ds(base, size), :]).T.astype(bf16)
        table = legc[pl.ds(base, size), :]
        base += size
        if c < len(cuts) - 1:
            sums = dot(weighted, table, ((1,), (0,)))
            partial[...] = sums if c == 0 else partial[...] + sums
            continue
        for p, (first, width) in enumerate(splits):
            cols = [slice(h * kq + first, h * kq + first + width) for h in range(2)]
            sums = dot(
                weighted, jnp.concatenate([table[:, q] for q in cols], axis=1), ((1,), (0,))
            )
            for h in range(2):
                mine = sums[:, h * width : (h + 1) * width]
                if c:
                    mine = mine + partial[:, cols[h]]
                tend = mine[: 2 * vl] + parity[:, cols[h]] * mine[2 * vl :]
                tend = (tend * (live[:, cols[h]] * time_step)).astype(bf16)
                for r in range(2):
                    tend_out[2 * r + h, :, first : first + width] = tend[r * vl : (r + 1) * vl]
            third.append(across(tend_out, tend_in, 2 + p))
    fourth = []
    for p, (start, count) in enumerate(splits):
        for cp in third[p]:
            cp.wait()
        change = tend_in[:, :, start : start + count].reshape(levs * vl, count)
        change = solve_change(change, damp[:, start : start + count])
        move_out[:, :, start : start + count] = change.reshape(levs, vl, count).astype(bf16)
        fourth.append(across(move_out, move_in, 2 + len(splits) + p))
    for cp in second:
        cp.wait()
    for p, (start, count) in enumerate(splits):
        for cp in fourth[p]:
            cp.wait()
        for r in range(2):
            for h in range(2):
                out_ref[:, r, h * kq + start : h * kq + start + count] = still_in[
                    2 * r + h, :, start : start + count
                ] + move_in[2 * r + h, :, start : start + count].astype(f32)
    for k, buf in ((0, to_grid), (1, to_slot)):
        for c in range(len(cuts)):
            await_all(buf, wave_send.at[k], c)


def local(
    spectral,
    legendre,
    gauss_weight,
    slot_waves,
    grid_factor,
    mode_projector,
    vertical_modes,
    mode_rates,
):
    _, vl, _, orders = spectral.shape
    half = legendre.shape[1]
    band, nlon = grid_factor.shape
    slots = slot_waves.shape[0]
    nmodes = mode_rates.shape[0]
    levs = nmodes // vl
    stride = ((orders - 1) // (slots - 1) - 1) // 2 * 2 + 1
    smooth, waves = tables(slots, nlon, stride)
    points = waves.shape[0]
    kq = orders // 2
    lanes = 128
    groups = lanes // vl
    tiles = band // groups
    first = tiles * 3 // 5
    cuts = ((0, first), (first, tiles - first))
    splits = ((0, kq),)
    cfg = (slots, levs, half, orders, nlon, band, stride, cuts, splits)
    swap = swap_blocks(groups, vl)
    vmem = pltpu.VMEM
    dma = pltpu.SemaphoreType.DMA
    cells = vmem((slots, tiles, 2, lanes), bf16)
    scratch = [
        vmem((vl, 2, orders), f32),
        vmem((half, orders), bf16),
        vmem((half,), f32),
        vmem((slots,), jnp.int32),
        pltpu.SMEM((slots,), jnp.int32),
        vmem((band, nlon), f32),
        vmem((nmodes, nmodes), f32),
        vmem((nmodes, nmodes), f32),
        vmem((nmodes,), f32),
        vmem(smooth.shape, bf16),
        vmem(waves.shape, bf16),
        vmem(swap.shape, bf16),
        dma((11,)),
        dma((5,)),
        dma((2,)),
        vmem((levs, vl, kq), f32),
        vmem((levs, vl, kq), f32),
        vmem((levs, vl, kq), f32),
        vmem((levs, vl, kq), f32),
        vmem((levs, vl, kq), bf16),
        vmem((levs, vl, kq), bf16),
        vmem((levs, vl, kq), bf16),
        vmem((levs, vl, kq), bf16),
        cells,
        cells,
        cells,
        cells,
        vmem((half, lanes), f32),
        vmem((half, lanes), f32),
        vmem((half, lanes), f32),
        vmem((half, lanes), f32),
        vmem((half, orders), bf16),
        vmem((4 * vl, orders), f32),
        vmem((nmodes, kq), f32),
        vmem((points, tiles * lanes), f32),
        vmem((points, 2 * slots), bf16),
        vmem((2 * slots, points), bf16),
        vmem((2, nmodes, 2 * nmodes), bf16),
        dma((2 + 2 * len(splits), levs - 1)),
        dma((2 + 2 * len(splits), levs - 1)),
        dma((2, len(cuts))),
        dma((2, len(cuts))),
    ]
    out = pl.pallas_call(
        functools.partial(kernel, cfg),
        out_shape=pltpu.VMEM((vl, 2, orders), f32),
        in_specs=[pl.BlockSpec(memory_space=pl.ANY)] * 11,
        out_specs=pl.BlockSpec(memory_space=vmem),
        scratch_shapes=scratch,
        compiler_params=pltpu.CompilerParams(
            collective_id=0, has_side_effects=True, vmem_limit_bytes=56 * 2**20
        ),
        name="round_trip",
    )(
        spectral[0],
        legendre[0],
        gauss_weight,
        slot_waves,
        grid_factor,
        mode_projector,
        vertical_modes,
        mode_rates,
        jnp.asarray(smooth),
        jnp.asarray(waves),
        jnp.asarray(swap),
    )
    return out[None]


def solution(mesh):
    in_specs = (
        P("wave", "lev", None, None),
        P("wave", None, None),
        P(),
        P(),
        P("wave", None),
        P(),
        P(),
        P(),
    )
    out_specs = P("wave", "lev", None, None)
    return jax.shard_map(local, mesh=mesh, in_specs=in_specs, out_specs=out_specs, check_vma=False)
```

```python
import functools
import math

import jax
import jax.numpy as jnp
import numpy as np
from jax import lax
from jax.experimental import pallas as pl
from jax.experimental.pallas import tpu as pltpu
from jax.sharding import PartitionSpec as P

time_step = 0.5
square_weight = 0.3
MESH = pl.DeviceIdType.MESH
f32, bf16 = jnp.float32, jnp.bfloat16
HIGHEST = lax.Precision.HIGHEST


@functools.lru_cache(maxsize=None)
def tables(slots, nlon, stride):
    points = 4 * slots
    step = nlon // points
    m = (np.arange(nlon, dtype=np.int64) * stride) % nlon
    i = np.arange(points, dtype=np.int64) * step
    q = np.arange(1, 2 * slots)
    series = 1.0 + 2.0 * np.cos(2.0 * np.pi * np.outer(np.arange(nlon), q) / nlon).sum(1)
    kernel = series[(m[None, :] - i[:, None]) % nlon] / nlon
    high = kernel.astype(np.float32).astype(jnp.bfloat16)
    low = (kernel - high.astype(np.float64)).astype(np.float32).astype(jnp.bfloat16)
    smooth = np.stack([part.T.reshape(nlon, -1, 128) for part in (high, low)], axis=1)
    smooth = np.ascontiguousarray(smooth.transpose(1, 2, 0, 3)).reshape(-1, nlon, 128)
    angle = 2.0 * np.pi * (np.outer(np.arange(points), np.arange(slots)) % points) / points
    waves = np.concatenate([np.cos(angle), -np.sin(angle)], axis=1)
    return smooth, waves.astype(np.float32).astype(jnp.bfloat16)


@functools.lru_cache(maxsize=None)
def swap_blocks(groups, size):
    width = groups * groups * size
    at = np.arange(width).reshape(groups, groups, size).transpose(1, 0, 2).reshape(-1)
    swap = np.zeros((width, width), np.float32)
    swap[at, np.arange(width)] = 1.0
    swap = swap.reshape(width, -1, 128).transpose(1, 0, 2)
    return np.ascontiguousarray(swap).astype(jnp.bfloat16)


def dot(a, b, contract, precision=None):
    return lax.dot_general(
        a, b, (contract, ((), ())), precision=precision, preferred_element_type=f32
    )


def kernel(
    cfg,
    spec_h,
    leg_h,
    gw_h,
    sw_h,
    fac_h,
    mp_h,
    vm_h,
    mr_h,
    smooth_h,
    waves_h,
    swap_h,
    out_ref,
    spec,
    leg,
    gw,
    sw,
    sw_s,
    fac,
    mp,
    vm,
    mr,
    smooth,
    waves,
    swap,
    in_sem,
    leg_sem,
    own_sem,
    mask_out,
    mask_in,
    still_out,
    still_in,
    tend_out,
    tend_in,
    move_out,
    move_in,
    to_grid,
    at_grid,
    to_slot,
    at_slot,
    field,
    rows32,
    gwb,
    gwbc,
    legc,
    partial,
    damp,
    fbig,
    trig,
    trig_t,
    pair,
    lev_send,
    lev_recv,
    wave_send,
    wave_recv,
):
    slots, levs, half, orders, nlon, band, stride, cuts, splits = cfg
    vl = spec.shape[0]
    lanes = 128
    groups = lanes // vl
    tiles = band // groups
    bands = half // band
    points = waves.shape[0]
    kq = orders // 2
    w = lax.axis_index("wave")
    y = lax.axis_index("lev")
    rows = 2 * tiles

    barrier = pltpu.get_barrier_semaphore()
    nx, nz = 4, slots // 8
    wx, wz, wc = lax.div(w, 2 * nz), lax.rem(lax.div(w, 2), nz), lax.rem(w, 2)

    def every_peer(act):
        for dz in (4, 5, 3, 6, 2, 7, 1, 0):
            first = (lax.rem(wz + dz, nz)) * 2
            shift = 2 if dz else 0

            def step(i, _):
                x = lax.rem(wx + shift + lax.div(i, 2), nx)
                act(x * (2 * nz) + first + lax.rem(wc + i, 2))
                return 0

            lax.fori_loop(0 if dz else 1, 2 * nx, step, 0, unroll=True)

    def greet(d):
        pl.semaphore_signal(barrier, inc=1, device_id=(d, y), device_id_type=MESH)

    every_peer(greet)
    for i in range(1, levs):
        pl.semaphore_signal(
            barrier, inc=1, device_id=(w, lax.rem(y + i, levs)), device_id_type=MESH
        )

    def load(src, dst, sem):
        cp = pltpu.make_async_copy(src, dst, sem)
        cp.start()
        return cp

    spec_cp = load(spec_h, spec, in_sem.at[0])
    swap_cp = load(swap_h, swap, in_sem.at[10])
    sws_cp = load(sw_h, sw_s, in_sem.at[1])
    pieces = 5
    piece = half // pieces
    leg_cps = [
        load(leg_h.at[pl.ds(i * piece, piece)], leg.at[pl.ds(i * piece, piece)], leg_sem.at[i])
        for i in range(pieces)
    ]
    others = [
        load(a, b, in_sem.at[2 + i])
        for i, (a, b) in enumerate(
            [
                (sw_h, sw),
                (waves_h, waves),
                (gw_h, gw),
                (mr_h, mr),
                (mp_h, mp),
                (vm_h, vm),
                (fac_h, fac),
                (smooth_h, smooth),
            ]
        )
    ]

    sws_cp.wait()
    spec_cp.wait()
    wave = sw_s[w] * stride
    order = lax.broadcasted_iota(jnp.int32, (1, orders), 1)
    live = jnp.where(order < orders - wave, 1.0, 0.0).astype(f32)
    parity = jnp.where(order % 2 == 0, 1.0, -1.0).astype(f32)
    masked = [spec[:, r, :] * live for r in range(2)]
    for r in range(2):
        for h in range(2):
            mask_out[2 * r + h] = masked[r][:, h * kq : (h + 1) * kq]
    coeffs = jnp.concatenate(masked, axis=0)
    coeffs = jnp.concatenate([coeffs, coeffs * parity], axis=0).astype(bf16)
    for i in range(pieces):
        leg_cps[i].wait()
        field[pl.ds(i * piece, piece), :] = dot(
            leg[pl.ds(i * piece, piece), :], coeffs, ((1,), (1,))
        )

    block = bands * tiles
    swap_cp.wait()

    def swapped(parts):
        turn = jnp.concatenate([swap[i] for i in range(groups)], axis=1)
        return dot(jnp.concatenate(parts, axis=1), turn, ((1,), (0,)))

    turned = swapped(
        [field[pl.ds(a, block, stride=groups), :].astype(bf16) for a in range(groups)]
    )
    for n in range(2):
        for r in range(2):
            q = 2 * n + r
            rows32[pl.ds(n * 2 * block + r, block, stride=2), :] = turned[
                :, q * lanes : (q + 1) * lanes
            ]
    to_grid[...] = rows32[...].astype(bf16).reshape(to_grid.shape)

    pl.semaphore_wait(barrier, slots - 1 + levs - 1)

    def place(d):
        return d + (d // bands) * (3 * bands - 1 - 2 * d)

    def forward(c, d):
        pltpu.make_async_remote_copy(
            src_ref=to_grid.at[place(d), pl.ds(*cuts[c])],
            dst_ref=at_grid.at[w, pl.ds(*cuts[c])],
            send_sem=wave_send.at[0, c],
            recv_sem=wave_recv.at[0, c],
            device_id=(d, y),
            device_id_type=MESH,
        ).start()

    for c in range(len(cuts)):
        every_peer(functools.partial(forward, c))
    own = pltpu.make_async_copy(to_grid.at[place(w)], at_grid.at[w], own_sem.at[0])
    own.start()

    def across(src, dst, k):
        cps = []
        for i in (2, 1, 3):
            to = lax.rem(y + i, levs)
            cp = pltpu.make_async_remote_copy(
                src_ref=src.at[to],
                dst_ref=dst.at[y],
                send_sem=lev_send.at[k, i - 1],
                recv_sem=lev_recv.at[k, i - 1],
                device_id=(w, to),
                device_id_type=MESH,
            )
            cp.start()
            cps.append(cp)
        dst[y] = src[y]
        return cps

    first = across(mask_out, mask_in, 0)

    for cp in others:
        cp.wait()
    for i in range(half // lanes):
        gwb[pl.ds(i * lanes, lanes), :] = jnp.broadcast_to(
            gw[pl.ds(i * lanes, lanes)].reshape(1, lanes), (lanes, lanes)
        ).T
    base = 0
    for start, count in cuts:
        size = count * groups
        for i in range(bands):
            src, dst = pl.ds(i * band + start * groups, size), pl.ds(base + i * size, size)
            legc[dst, :] = leg[src, :]
            gwbc[dst, :] = gwb[src, :]
        base += bands * size
    part_j = lax.broadcasted_iota(jnp.int32, (2 * slots, slots), 0)
    held = jnp.broadcast_to(sw[...].reshape(1, slots), (2 * slots, slots))
    choose = jnp.concatenate(
        [jnp.where(part_j == held + r * slots, 1.0, 0.0) for r in range(2)], axis=1
    ).astype(bf16)
    turned = dot(waves[...], choose, ((1,), (0,)))
    trig[...] = turned.astype(bf16)
    trig_t[...] = turned.T.astype(bf16)

    factor = fac[...]
    fhigh = factor.astype(bf16)
    flow = (factor - fhigh.astype(f32)).astype(bf16)
    half_points = points // lanes
    shigh, slow = [
        jnp.concatenate([smooth[n * half_points + i] for i in range(half_points)], axis=1)
        for n in range(2)
    ]
    top = dot(fhigh, shigh, ((1,), (0,))) + dot(flow, shigh, ((1,), (0,)))
    top += dot(fhigh, slow, ((1,), (0,)))
    root = 1.0 / math.sqrt(slots)
    top = top * root
    thigh = top.astype(bf16)
    tlow = (top - thigh.astype(f32)).astype(bf16)
    row = lax.broadcasted_iota(jnp.int32, (band, tiles * lanes), 0)
    south = w // bands
    row = row + south * (band - 1 - 2 * row)
    col = lax.broadcasted_iota(jnp.int32, (band, tiles * lanes), 1) // vl
    spread = jnp.where(row == col, 1.0, 0.0).astype(bf16)
    fbig[...] = dot(thigh, spread, ((0,), (0,))) + dot(tlow, spread, ((0,), (0,)))

    total = (wave + (y % 2) * kq + lax.broadcasted_iota(jnp.int32, (1, kq), 1)).astype(f32)
    damping = total * (total + 1.0) / float(orders * orders)
    rates = jnp.broadcast_to(mr[...].reshape(1, lanes), (lanes, lanes)).T[:, :1]
    damp[...] = 1.0 / (1.0 + rates * damping)

    def solve(x):
        modes = dot(mp[...], x, ((1,), (0,)), HIGHEST) * damp[...]
        return dot(vm[...], modes, ((1,), (0,)), HIGHEST)

    def split(x):
        high = x.astype(bf16)
        return high, (x - high.astype(f32)).astype(bf16)

    ends = [split(ref[...]) for ref in (mp, vm)]
    for k in range(2):
        pair[k] = jnp.concatenate(ends[k], axis=1)

    def solve_change(x, damping):
        modes = dot(pair[0], jnp.concatenate([x, x], axis=0), ((1,), (0,))) * damping
        high, low = split(modes)
        out = dot(pair[1], jnp.concatenate([high, high], axis=0), ((1,), (0,)))
        return out + dot(pair[1, :, :lanes], low, ((1,), (0,)))

    for cp in first:
        cp.wait()
    still_out[...] = solve(mask_in[...].reshape(levs * vl, kq)).reshape(levs, vl, kq)
    second = across(still_out, still_in, 1)

    def await_all(buf, sems, c):
        ref = buf.at[pl.ds(0, slots - 1), pl.ds(*cuts[c])]
        pltpu.make_async_copy(ref, ref, sems.at[c]).wait()

    def backward(c, d):
        pltpu.make_async_remote_copy(
            src_ref=to_slot.at[d, pl.ds(*cuts[c])],
            dst_ref=at_slot.at[place(w), pl.ds(*cuts[c])],
            send_sem=wave_send.at[1, c],
            recv_sem=wave_recv.at[1, c],
            device_id=(d, y),
            device_id_type=MESH,
        ).start()

    own.wait()
    for c, (start, count) in enumerate(cuts):
        await_all(at_grid, wave_recv.at[0], c)
        chunk = 2 * count
        here = pl.ds(0, slots * chunk)
        rows32[here, :] = (
            at_grid[:, start : start + count].reshape(slots * chunk, lanes).astype(f32)
        )
        parts = jnp.concatenate(
            [
                jnp.concatenate(
                    [rows32[pl.ds(2 * u + r, slots, stride=chunk), :] for r in range(2)], axis=0
                ).astype(bf16)
                for u in range(count)
            ],
            axis=1,
        )
        grid = dot(trig[...], parts, ((1,), (0,)))
        scaled = fbig[:, start * lanes : (start + count) * lanes]
        product = (grid * (scaled + (square_weight * root * root) * grid)).astype(bf16)
        back = dot(trig_t[...], product, ((1,), (0,)))
        back = back * ((nlon // points) / math.sqrt(nlon))
        for u in range(count):
            for r in range(2):
                field[pl.ds(2 * u + r, slots, stride=chunk), :] = back[
                    r * slots : (r + 1) * slots, u * lanes : (u + 1) * lanes
                ]
        to_slot[:, start : start + count] = (
            field[here, :].astype(bf16).reshape(slots, count, 2, lanes)
        )
        every_peer(functools.partial(backward, c))
    own = pltpu.make_async_copy(to_slot.at[w], at_slot.at[place(w)], own_sem.at[1])
    own.start()
    own.wait()
    third = []
    base = 0
    for c, (start, count) in enumerate(cuts):
        await_all(at_slot, wave_recv.at[1], c)
        size = bands * count * groups
        some = bands * count
        rows32[pl.ds(0, slots * 2 * count), :] = (
            at_slot[:, start : start + count].reshape(slots * 2 * count, lanes).astype(f32)
        )
        turned = swapped(
            [
                rows32[pl.ds(n * 2 * some + r, some, stride=2), :].astype(bf16)
                for n in range(2)
                for r in range(2)
            ]
        )
        for a in range(groups):
            field[pl.ds(a, some, stride=groups), :] = turned[:, a * lanes : (a + 1) * lanes]
        weighted = (field[pl.ds(0, size), :] * gwbc[pl.ds(base, size), :]).T.astype(bf16)
        table = legc[pl.ds(base, size), :]
        base += size
        if c < len(cuts) - 1:
            sums = dot(weighted, table, ((1,), (0,)))
            partial[...] = sums if c == 0 else partial[...] + sums
            continue
        for p, (first, width) in enumerate(splits):
            cols = [slice(h * kq + first, h * kq + first + width) for h in range(2)]
            sums = dot(
                weighted, jnp.concatenate([table[:, q] for q in cols], axis=1), ((1,), (0,))
            )
            for h in range(2):
                mine = sums[:, h * width : (h + 1) * width]
                if c:
                    mine = mine + partial[:, cols[h]]
                tend = mine[: 2 * vl] + parity[:, cols[h]] * mine[2 * vl :]
                tend = (tend * (live[:, cols[h]] * time_step)).astype(bf16)
                for r in range(2):
                    tend_out[2 * r + h, :, first : first + width] = tend[r * vl : (r + 1) * vl]
            third.append(across(tend_out, tend_in, 2 + p))
    fourth = []
    for p, (start, count) in enumerate(splits):
        for cp in third[p]:
            cp.wait()
        change = tend_in[:, :, start : start + count].reshape(levs * vl, count)
        change = solve_change(change, damp[:, start : start + count])
        move_out[:, :, start : start + count] = change.reshape(levs, vl, count).astype(bf16)
        fourth.append(across(move_out, move_in, 2 + len(splits) + p))
    for cp in second:
        cp.wait()
    for p, (start, count) in enumerate(splits):
        for cp in fourth[p]:
            cp.wait()
        for r in range(2):
            for h in range(2):
                out_ref[:, r, h * kq + start : h * kq + start + count] = still_in[
                    2 * r + h, :, start : start + count
                ] + move_in[2 * r + h, :, start : start + count].astype(f32)
    for k, buf in ((0, to_grid), (1, to_slot)):
        for c in range(len(cuts)):
            await_all(buf, wave_send.at[k], c)


def local(
    spectral,
    legendre,
    gauss_weight,
    slot_waves,
    grid_factor,
    mode_projector,
    vertical_modes,
    mode_rates,
):
    _, vl, _, orders = spectral.shape
    half = legendre.shape[1]
    band, nlon = grid_factor.shape
    slots = slot_waves.shape[0]
    nmodes = mode_rates.shape[0]
    levs = nmodes // vl
    stride = ((orders - 1) // (slots - 1) - 1) // 2 * 2 + 1
    smooth, waves = tables(slots, nlon, stride)
    points = waves.shape[0]
    kq = orders // 2
    lanes = 128
    groups = lanes // vl
    tiles = band // groups
    first = tiles // 2
    cuts = ((0, first), (first, tiles - first))
    splits = ((0, kq),)
    cfg = (slots, levs, half, orders, nlon, band, stride, cuts, splits)
    swap = swap_blocks(groups, vl)
    vmem = pltpu.VMEM
    dma = pltpu.SemaphoreType.DMA
    cells = vmem((slots, tiles, 2, lanes), bf16)
    scratch = [
        vmem((vl, 2, orders), f32),
        vmem((half, orders), bf16),
        vmem((half,), f32),
        vmem((slots,), jnp.int32),
        pltpu.SMEM((slots,), jnp.int32),
        vmem((band, nlon), f32),
        vmem((nmodes, nmodes), f32),
        vmem((nmodes, nmodes), f32),
        vmem((nmodes,), f32),
        vmem(smooth.shape, bf16),
        vmem(waves.shape, bf16),
        vmem(swap.shape, bf16),
        dma((11,)),
        dma((5,)),
        dma((2,)),
        vmem((levs, vl, kq), f32),
        vmem((levs, vl, kq), f32),
        vmem((levs, vl, kq), f32),
        vmem((levs, vl, kq), f32),
        vmem((levs, vl, kq), bf16),
        vmem((levs, vl, kq), bf16),
        vmem((levs, vl, kq), bf16),
        vmem((levs, vl, kq), bf16),
        cells,
        cells,
        cells,
        cells,
        vmem((half, lanes), f32),
        vmem((half, lanes), f32),
        vmem((half, lanes), f32),
        vmem((half, lanes), f32),
        vmem((half, orders), bf16),
        vmem((4 * vl, orders), f32),
        vmem((nmodes, kq), f32),
        vmem((points, tiles * lanes), f32),
        vmem((points, 2 * slots), bf16),
        vmem((2 * slots, points), bf16),
        vmem((2, nmodes, 2 * nmodes), bf16),
        dma((2 + 2 * len(splits), levs - 1)),
        dma((2 + 2 * len(splits), levs - 1)),
        dma((2, len(cuts))),
        dma((2, len(cuts))),
    ]
    out = pl.pallas_call(
        functools.partial(kernel, cfg),
        out_shape=pltpu.VMEM((vl, 2, orders), f32),
        in_specs=[pl.BlockSpec(memory_space=pl.ANY)] * 11,
        out_specs=pl.BlockSpec(memory_space=vmem),
        scratch_shapes=scratch,
        compiler_params=pltpu.CompilerParams(
            collective_id=0, has_side_effects=True, vmem_limit_bytes=56 * 2**20
        ),
        name="round_trip",
    )(
        spectral[0],
        legendre[0],
        gauss_weight,
        slot_waves,
        grid_factor,
        mode_projector,
        vertical_modes,
        mode_rates,
        jnp.asarray(smooth),
        jnp.asarray(waves),
        jnp.asarray(swap),
    )
    return out[None]


def solution(mesh):
    in_specs = (
        P("wave", "lev", None, None),
        P("wave", None, None),
        P(),
        P(),
        P("wave", None),
        P(),
        P(),
        P(),
    )
    out_specs = P("wave", "lev", None, None)
    return jax.shard_map(local, mesh=mesh, in_specs=in_specs, out_specs=out_specs, check_vma=False)
```

```python
import functools
import math

import jax
import jax.numpy as jnp
import numpy as np
from jax import lax
from jax.experimental import pallas as pl
from jax.experimental.pallas import tpu as pltpu
from jax.sharding import PartitionSpec as P

time_step = 0.5
square_weight = 0.3
MESH = pl.DeviceIdType.MESH
f32, bf16 = jnp.float32, jnp.bfloat16
HIGHEST = lax.Precision.HIGHEST


@functools.lru_cache(maxsize=None)
def tables(slots, nlon, stride):
    points = 4 * slots
    step = nlon // points
    m = (np.arange(nlon, dtype=np.int64) * stride) % nlon
    i = np.arange(points, dtype=np.int64) * step
    q = np.arange(1, 2 * slots)
    series = 1.0 + 2.0 * np.cos(2.0 * np.pi * np.outer(np.arange(nlon), q) / nlon).sum(1)
    kernel = series[(m[None, :] - i[:, None]) % nlon] / nlon
    high = kernel.astype(np.float32).astype(jnp.bfloat16)
    low = (kernel - high.astype(np.float64)).astype(np.float32).astype(jnp.bfloat16)
    smooth = np.stack([part.T.reshape(nlon, -1, 128) for part in (high, low)], axis=1)
    smooth = np.ascontiguousarray(smooth.transpose(1, 2, 0, 3)).reshape(-1, nlon, 128)
    angle = 2.0 * np.pi * (np.outer(np.arange(points), np.arange(slots)) % points) / points
    waves = np.concatenate([np.cos(angle), -np.sin(angle)], axis=1)
    return smooth, waves.astype(np.float32).astype(jnp.bfloat16)


@functools.lru_cache(maxsize=None)
def swap_blocks(groups, size):
    width = groups * groups * size
    at = np.arange(width).reshape(groups, groups, size).transpose(1, 0, 2).reshape(-1)
    swap = np.zeros((width, width), np.float32)
    swap[at, np.arange(width)] = 1.0
    swap = swap.reshape(width, -1, 128).transpose(1, 0, 2)
    return np.ascontiguousarray(swap).astype(jnp.bfloat16)


def dot(a, b, contract, precision=None):
    return lax.dot_general(
        a, b, (contract, ((), ())), precision=precision, preferred_element_type=f32
    )


def kernel(
    cfg,
    spec_h,
    leg_h,
    gw_h,
    sw_h,
    fac_h,
    mp_h,
    vm_h,
    mr_h,
    smooth_h,
    waves_h,
    swap_h,
    out_ref,
    spec,
    leg,
    gw,
    sw,
    sw_s,
    fac,
    mp,
    vm,
    mr,
    smooth,
    waves,
    swap,
    in_sem,
    leg_sem,
    own_sem,
    mask_out,
    mask_in,
    still_out,
    still_in,
    tend_out,
    tend_in,
    move_out,
    move_in,
    to_grid,
    at_grid,
    to_slot,
    at_slot,
    field,
    rows32,
    gwb,
    gwbc,
    legc,
    partial,
    damp,
    fbig,
    trig,
    trig_t,
    pair,
    lev_send,
    lev_recv,
    wave_send,
    wave_recv,
):
    slots, levs, half, orders, nlon, band, stride, cuts, splits = cfg
    vl = spec.shape[0]
    lanes = 128
    groups = lanes // vl
    tiles = band // groups
    bands = half // band
    points = waves.shape[0]
    kq = orders // 2
    w = lax.axis_index("wave")
    y = lax.axis_index("lev")
    rows = 2 * tiles

    barrier = pltpu.get_barrier_semaphore()
    nx, nz = 4, slots // 8
    wx, wz, wc = lax.div(w, 2 * nz), lax.rem(lax.div(w, 2), nz), lax.rem(w, 2)

    def every_peer(act):
        for dx in (2, 1, 3, 0):
            for dz in (4, 5, 3, 6, 2, 7, 1, 0):
                first = lax.rem(wx + dx, nx) * (2 * nz) + lax.rem(wz + dz, nz) * 2
                for core in range(2):
                    if dx or dz or core:
                        act(first + lax.rem(wc + core, 2))

    def greet(d):
        pl.semaphore_signal(barrier, inc=1, device_id=(d, y), device_id_type=MESH)

    every_peer(greet)
    for i in range(1, levs):
        pl.semaphore_signal(
            barrier, inc=1, device_id=(w, lax.rem(y + i, levs)), device_id_type=MESH
        )

    def load(src, dst, sem):
        cp = pltpu.make_async_copy(src, dst, sem)
        cp.start()
        return cp

    spec_cp = load(spec_h, spec, in_sem.at[0])
    swap_cp = load(swap_h, swap, in_sem.at[10])
    sws_cp = load(sw_h, sw_s, in_sem.at[1])
    pieces = 5
    piece = half // pieces
    leg_cps = [
        load(leg_h.at[pl.ds(i * piece, piece)], leg.at[pl.ds(i * piece, piece)], leg_sem.at[i])
        for i in range(pieces)
    ]
    others = [
        load(a, b, in_sem.at[2 + i])
        for i, (a, b) in enumerate(
            [
                (sw_h, sw),
                (waves_h, waves),
                (gw_h, gw),
                (mr_h, mr),
                (mp_h, mp),
                (vm_h, vm),
                (fac_h, fac),
                (smooth_h, smooth),
            ]
        )
    ]

    sws_cp.wait()
    spec_cp.wait()
    wave = sw_s[w] * stride
    order = lax.broadcasted_iota(jnp.int32, (1, orders), 1)
    live = jnp.where(order < orders - wave, 1.0, 0.0).astype(f32)
    parity = jnp.where(order % 2 == 0, 1.0, -1.0).astype(f32)
    masked = [spec[:, r, :] * live for r in range(2)]
    for r in range(2):
        for h in range(2):
            mask_out[2 * r + h] = masked[r][:, h * kq : (h + 1) * kq]
    coeffs = jnp.concatenate(masked, axis=0)
    coeffs = jnp.concatenate([coeffs, coeffs * parity], axis=0).astype(bf16)
    for i in range(pieces):
        leg_cps[i].wait()
        field[pl.ds(i * piece, piece), :] = dot(
            leg[pl.ds(i * piece, piece), :], coeffs, ((1,), (1,))
        )

    block = bands * tiles
    swap_cp.wait()

    def swapped(parts):
        turn = jnp.concatenate([swap[i] for i in range(groups)], axis=1)
        return dot(jnp.concatenate(parts, axis=1), turn, ((1,), (0,)))

    turned = swapped(
        [field[pl.ds(a, block, stride=groups), :].astype(bf16) for a in range(groups)]
    )
    for n in range(2):
        for r in range(2):
            q = 2 * n + r
            rows32[pl.ds(n * 2 * block + r, block, stride=2), :] = turned[
                :, q * lanes : (q + 1) * lanes
            ]
    to_grid[...] = rows32[...].astype(bf16).reshape(to_grid.shape)

    pl.semaphore_wait(barrier, slots - 1 + levs - 1)

    def place(d):
        return d + (d // bands) * (3 * bands - 1 - 2 * d)

    def forward(c, d):
        pltpu.make_async_remote_copy(
            src_ref=to_grid.at[place(d), pl.ds(*cuts[c])],
            dst_ref=at_grid.at[w, pl.ds(*cuts[c])],
            send_sem=wave_send.at[0, c],
            recv_sem=wave_recv.at[0, c],
            device_id=(d, y),
            device_id_type=MESH,
        ).start()

    for c in range(len(cuts)):
        every_peer(functools.partial(forward, c))
    own = pltpu.make_async_copy(to_grid.at[place(w)], at_grid.at[w], own_sem.at[0])
    own.start()

    def across(src, dst, k):
        cps = []
        for i in (2, 1, 3):
            to = lax.rem(y + i, levs)
            cp = pltpu.make_async_remote_copy(
                src_ref=src.at[to],
                dst_ref=dst.at[y],
                send_sem=lev_send.at[k, i - 1],
                recv_sem=lev_recv.at[k, i - 1],
                device_id=(w, to),
                device_id_type=MESH,
            )
            cp.start()
            cps.append(cp)
        dst[y] = src[y]
        return cps

    first = across(mask_out, mask_in, 0)

    for cp in others:
        cp.wait()
    for i in range(half // lanes):
        gwb[pl.ds(i * lanes, lanes), :] = jnp.broadcast_to(
            gw[pl.ds(i * lanes, lanes)].reshape(1, lanes), (lanes, lanes)
        ).T
    base = 0
    for start, count in cuts:
        size = count * groups
        for i in range(bands):
            src, dst = pl.ds(i * band + start * groups, size), pl.ds(base + i * size, size)
            legc[dst, :] = leg[src, :]
            gwbc[dst, :] = gwb[src, :]
        base += bands * size
    part_j = lax.broadcasted_iota(jnp.int32, (2 * slots, slots), 0)
    held = jnp.broadcast_to(sw[...].reshape(1, slots), (2 * slots, slots))
    choose = jnp.concatenate(
        [jnp.where(part_j == held + r * slots, 1.0, 0.0) for r in range(2)], axis=1
    ).astype(bf16)
    turned = dot(waves[...], choose, ((1,), (0,)))
    trig[...] = turned.astype(bf16)
    trig_t[...] = turned.T.astype(bf16)

    factor = fac[...]
    fhigh = factor.astype(bf16)
    flow = (factor - fhigh.astype(f32)).astype(bf16)
    half_points = points // lanes
    shigh, slow = [
        jnp.concatenate([smooth[n * half_points + i] for i in range(half_points)], axis=1)
        for n in range(2)
    ]
    top = dot(fhigh, shigh, ((1,), (0,))) + dot(flow, shigh, ((1,), (0,)))
    top += dot(fhigh, slow, ((1,), (0,)))
    root = 1.0 / math.sqrt(slots)
    top = top * root
    thigh = top.astype(bf16)
    tlow = (top - thigh.astype(f32)).astype(bf16)
    row = lax.broadcasted_iota(jnp.int32, (band, tiles * lanes), 0)
    south = w // bands
    row = row + south * (band - 1 - 2 * row)
    col = lax.broadcasted_iota(jnp.int32, (band, tiles * lanes), 1) // vl
    spread = jnp.where(row == col, 1.0, 0.0).astype(bf16)
    fbig[...] = dot(thigh, spread, ((0,), (0,))) + dot(tlow, spread, ((0,), (0,)))

    total = (wave + (y % 2) * kq + lax.broadcasted_iota(jnp.int32, (1, kq), 1)).astype(f32)
    damping = total * (total + 1.0) / float(orders * orders)
    rates = jnp.broadcast_to(mr[...].reshape(1, lanes), (lanes, lanes)).T[:, :1]
    damp[...] = 1.0 / (1.0 + rates * damping)

    def solve(x):
        modes = dot(mp[...], x, ((1,), (0,)), HIGHEST) * damp[...]
        return dot(vm[...], modes, ((1,), (0,)), HIGHEST)

    def split(x):
        high = x.astype(bf16)
        return high, (x - high.astype(f32)).astype(bf16)

    ends = [split(ref[...]) for ref in (mp, vm)]
    for k in range(2):
        pair[k] = jnp.concatenate(ends[k], axis=1)

    def solve_change(x, damping):
        modes = dot(pair[0], jnp.concatenate([x, x], axis=0), ((1,), (0,))) * damping
        high, low = split(modes)
        out = dot(pair[1], jnp.concatenate([high, high], axis=0), ((1,), (0,)))
        return out + dot(pair[1, :, :lanes], low, ((1,), (0,)))

    for cp in first:
        cp.wait()
    still_out[...] = solve(mask_in[...].reshape(levs * vl, kq)).reshape(levs, vl, kq)
    second = across(still_out, still_in, 1)

    def await_all(buf, sems, c):
        ref = buf.at[pl.ds(0, slots - 1), pl.ds(*cuts[c])]
        pltpu.make_async_copy(ref, ref, sems.at[c]).wait()

    def backward(c, d):
        pltpu.make_async_remote_copy(
            src_ref=to_slot.at[d, pl.ds(*cuts[c])],
            dst_ref=at_slot.at[place(w), pl.ds(*cuts[c])],
            send_sem=wave_send.at[1, c],
            recv_sem=wave_recv.at[1, c],
            device_id=(d, y),
            device_id_type=MESH,
        ).start()

    own.wait()
    for c, (start, count) in enumerate(cuts):
        await_all(at_grid, wave_recv.at[0], c)
        chunk = 2 * count
        here = pl.ds(0, slots * chunk)
        rows32[here, :] = (
            at_grid[:, start : start + count].reshape(slots * chunk, lanes).astype(f32)
        )
        parts = jnp.concatenate(
            [
                jnp.concatenate(
                    [rows32[pl.ds(2 * u + r, slots, stride=chunk), :] for r in range(2)], axis=0
                ).astype(bf16)
                for u in range(count)
            ],
            axis=1,
        )
        grid = dot(trig[...], parts, ((1,), (0,)))
        scaled = fbig[:, start * lanes : (start + count) * lanes]
        product = (grid * (scaled + (square_weight * root * root) * grid)).astype(bf16)
        back = dot(trig_t[...], product, ((1,), (0,)))
        back = back * ((nlon // points) / math.sqrt(nlon))
        for u in range(count):
            for r in range(2):
                field[pl.ds(2 * u + r, slots, stride=chunk), :] = back[
                    r * slots : (r + 1) * slots, u * lanes : (u + 1) * lanes
                ]
        to_slot[:, start : start + count] = (
            field[here, :].astype(bf16).reshape(slots, count, 2, lanes)
        )
        every_peer(functools.partial(backward, c))
    own = pltpu.make_async_copy(to_slot.at[w], at_slot.at[place(w)], own_sem.at[1])
    own.start()
    own.wait()
    third = []
    base = 0
    for c, (start, count) in enumerate(cuts):
        await_all(at_slot, wave_recv.at[1], c)
        size = bands * count * groups
        some = bands * count
        rows32[pl.ds(0, slots * 2 * count), :] = (
            at_slot[:, start : start + count].reshape(slots * 2 * count, lanes).astype(f32)
        )
        turned = swapped(
            [
                rows32[pl.ds(n * 2 * some + r, some, stride=2), :].astype(bf16)
                for n in range(2)
                for r in range(2)
            ]
        )
        for a in range(groups):
            field[pl.ds(a, some, stride=groups), :] = turned[:, a * lanes : (a + 1) * lanes]
        weighted = (field[pl.ds(0, size), :] * gwbc[pl.ds(base, size), :]).T.astype(bf16)
        table = legc[pl.ds(base, size), :]
        base += size
        if c < len(cuts) - 1:
            sums = dot(weighted, table, ((1,), (0,)))
            partial[...] = sums if c == 0 else partial[...] + sums
            continue
        for p, (first, width) in enumerate(splits):
            cols = [slice(h * kq + first, h * kq + first + width) for h in range(2)]
            sums = dot(
                weighted, jnp.concatenate([table[:, q] for q in cols], axis=1), ((1,), (0,))
            )
            for h in range(2):
                mine = sums[:, h * width : (h + 1) * width]
                if c:
                    mine = mine + partial[:, cols[h]]
                tend = mine[: 2 * vl] + parity[:, cols[h]] * mine[2 * vl :]
                tend = (tend * (live[:, cols[h]] * time_step)).astype(bf16)
                for r in range(2):
                    tend_out[2 * r + h, :, first : first + width] = tend[r * vl : (r + 1) * vl]
            third.append(across(tend_out, tend_in, 2 + p))
    fourth = []
    for p, (start, count) in enumerate(splits):
        for cp in third[p]:
            cp.wait()
        change = tend_in[:, :, start : start + count].reshape(levs * vl, count)
        change = solve_change(change, damp[:, start : start + count])
        move_out[:, :, start : start + count] = change.reshape(levs, vl, count).astype(bf16)
        fourth.append(across(move_out, move_in, 2 + len(splits) + p))
    for cp in second:
        cp.wait()
    for p, (start, count) in enumerate(splits):
        for cp in fourth[p]:
            cp.wait()
        for r in range(2):
            for h in range(2):
                out_ref[:, r, h * kq + start : h * kq + start + count] = still_in[
                    2 * r + h, :, start : start + count
                ] + move_in[2 * r + h, :, start : start + count].astype(f32)
    for k, buf in ((0, to_grid), (1, to_slot)):
        for c in range(len(cuts)):
            await_all(buf, wave_send.at[k], c)


def local(
    spectral,
    legendre,
    gauss_weight,
    slot_waves,
    grid_factor,
    mode_projector,
    vertical_modes,
    mode_rates,
):
    _, vl, _, orders = spectral.shape
    half = legendre.shape[1]
    band, nlon = grid_factor.shape
    slots = slot_waves.shape[0]
    nmodes = mode_rates.shape[0]
    levs = nmodes // vl
    stride = ((orders - 1) // (slots - 1) - 1) // 2 * 2 + 1
    smooth, waves = tables(slots, nlon, stride)
    points = waves.shape[0]
    kq = orders // 2
    lanes = 128
    groups = lanes // vl
    tiles = band // groups
    first = tiles // 2
    cuts = ((0, first), (first, tiles - first))
    splits = ((0, kq),)
    cfg = (slots, levs, half, orders, nlon, band, stride, cuts, splits)
    swap = swap_blocks(groups, vl)
    vmem = pltpu.VMEM
    dma = pltpu.SemaphoreType.DMA
    cells = vmem((slots, tiles, 2, lanes), bf16)
    scratch = [
        vmem((vl, 2, orders), f32),
        vmem((half, orders), bf16),
        vmem((half,), f32),
        vmem((slots,), jnp.int32),
        pltpu.SMEM((slots,), jnp.int32),
        vmem((band, nlon), f32),
        vmem((nmodes, nmodes), f32),
        vmem((nmodes, nmodes), f32),
        vmem((nmodes,), f32),
        vmem(smooth.shape, bf16),
        vmem(waves.shape, bf16),
        vmem(swap.shape, bf16),
        dma((11,)),
        dma((5,)),
        dma((2,)),
        vmem((levs, vl, kq), f32),
        vmem((levs, vl, kq), f32),
        vmem((levs, vl, kq), f32),
        vmem((levs, vl, kq), f32),
        vmem((levs, vl, kq), bf16),
        vmem((levs, vl, kq), bf16),
        vmem((levs, vl, kq), bf16),
        vmem((levs, vl, kq), bf16),
        cells,
        cells,
        cells,
        cells,
        vmem((half, lanes), f32),
        vmem((half, lanes), f32),
        vmem((half, lanes), f32),
        vmem((half, lanes), f32),
        vmem((half, orders), bf16),
        vmem((4 * vl, orders), f32),
        vmem((nmodes, kq), f32),
        vmem((points, tiles * lanes), f32),
        vmem((points, 2 * slots), bf16),
        vmem((2 * slots, points), bf16),
        vmem((2, nmodes, 2 * nmodes), bf16),
        dma((2 + 2 * len(splits), levs - 1)),
        dma((2 + 2 * len(splits), levs - 1)),
        dma((2, len(cuts))),
        dma((2, len(cuts))),
    ]
    out = pl.pallas_call(
        functools.partial(kernel, cfg),
        out_shape=pltpu.VMEM((vl, 2, orders), f32),
        in_specs=[pl.BlockSpec(memory_space=pl.ANY)] * 11,
        out_specs=pl.BlockSpec(memory_space=vmem),
        scratch_shapes=scratch,
        compiler_params=pltpu.CompilerParams(
            collective_id=0, has_side_effects=True, vmem_limit_bytes=56 * 2**20
        ),
        name="round_trip",
    )(
        spectral[0],
        legendre[0],
        gauss_weight,
        slot_waves,
        grid_factor,
        mode_projector,
        vertical_modes,
        mode_rates,
        jnp.asarray(smooth),
        jnp.asarray(waves),
        jnp.asarray(swap),
    )
    return out[None]


def solution(mesh):
    in_specs = (
        P("wave", "lev", None, None),
        P("wave", None, None),
        P(),
        P(),
        P("wave", None),
        P(),
        P(),
        P(),
    )
    out_specs = P("wave", "lev", None, None)
    return jax.shard_map(local, mesh=mesh, in_specs=in_specs, out_specs=out_specs, check_vma=False)
```

```python
import functools
import math

import jax
import jax.numpy as jnp
import numpy as np
from jax import lax
from jax.experimental import pallas as pl
from jax.experimental.pallas import tpu as pltpu
from jax.sharding import PartitionSpec as P

time_step = 0.5
square_weight = 0.3
MESH = pl.DeviceIdType.MESH
f32, bf16 = jnp.float32, jnp.bfloat16
HIGHEST = lax.Precision.HIGHEST


@functools.lru_cache(maxsize=None)
def tables(slots, nlon, stride):
    points = 4 * slots
    step = nlon // points
    m = (np.arange(nlon, dtype=np.int64) * stride) % nlon
    i = np.arange(points, dtype=np.int64) * step
    q = np.arange(1, 2 * slots)
    series = 1.0 + 2.0 * np.cos(2.0 * np.pi * np.outer(np.arange(nlon), q) / nlon).sum(1)
    kernel = series[(m[None, :] - i[:, None]) % nlon] / nlon
    high = kernel.astype(np.float32).astype(jnp.bfloat16)
    low = (kernel - high.astype(np.float64)).astype(np.float32).astype(jnp.bfloat16)
    smooth = np.stack([part.T.reshape(nlon, -1, 128) for part in (high, low)], axis=1)
    smooth = np.ascontiguousarray(smooth.transpose(1, 2, 0, 3)).reshape(-1, nlon, 128)
    angle = 2.0 * np.pi * (np.outer(np.arange(points), np.arange(slots)) % points) / points
    waves = np.concatenate([np.cos(angle), -np.sin(angle)], axis=1)
    return smooth, waves.astype(np.float32).astype(jnp.bfloat16)


@functools.lru_cache(maxsize=None)
def swap_blocks(groups, size):
    width = groups * groups * size
    at = np.arange(width).reshape(groups, groups, size).transpose(1, 0, 2).reshape(-1)
    swap = np.zeros((width, width), np.float32)
    swap[at, np.arange(width)] = 1.0
    swap = swap.reshape(width, -1, 128).transpose(1, 0, 2)
    return np.ascontiguousarray(swap).astype(jnp.bfloat16)


def dot(a, b, contract, precision=None):
    return lax.dot_general(
        a, b, (contract, ((), ())), precision=precision, preferred_element_type=f32
    )


def kernel(
    cfg,
    spec_h,
    leg_h,
    gw_h,
    sw_h,
    fac_h,
    mp_h,
    vm_h,
    mr_h,
    smooth_h,
    waves_h,
    swap_h,
    out_ref,
    spec,
    leg,
    gw,
    sw,
    sw_s,
    fac,
    mp,
    vm,
    mr,
    smooth,
    waves,
    swap,
    in_sem,
    leg_sem,
    own_sem,
    mask_out,
    mask_in,
    still_out,
    still_in,
    tend_out,
    tend_in,
    move_out,
    move_in,
    to_grid,
    at_grid,
    to_slot,
    at_slot,
    field,
    rows32,
    gwb,
    gwbc,
    legc,
    partial,
    damp,
    fbig,
    trig,
    trig_t,
    pair,
    lev_send,
    lev_recv,
    wave_send,
    wave_recv,
):
    slots, levs, half, orders, nlon, band, stride, cuts, splits = cfg
    vl = spec.shape[0]
    lanes = 128
    groups = lanes // vl
    tiles = band // groups
    bands = half // band
    points = waves.shape[0]
    kq = orders // 2
    w = lax.axis_index("wave")
    y = lax.axis_index("lev")
    rows = 2 * tiles

    barrier = pltpu.get_barrier_semaphore()
    nx, nz = 4, slots // 8
    wx, wz, wc = lax.div(w, 2 * nz), lax.rem(lax.div(w, 2), nz), lax.rem(w, 2)

    def every_peer(act):
        for dx in (2, 1, 3, 0):
            for dz in (4, 3, 5, 2, 6, 1, 7, 0):
                first = lax.rem(wx + dx, nx) * (2 * nz) + lax.rem(wz + dz, nz) * 2
                for core in range(2):
                    if dx or dz or core:
                        act(first + lax.rem(wc + core, 2))

    def greet(d):
        pl.semaphore_signal(barrier, inc=1, device_id=(d, y), device_id_type=MESH)

    every_peer(greet)
    for i in range(1, levs):
        pl.semaphore_signal(
            barrier, inc=1, device_id=(w, lax.rem(y + i, levs)), device_id_type=MESH
        )

    def load(src, dst, sem):
        cp = pltpu.make_async_copy(src, dst, sem)
        cp.start()
        return cp

    spec_cp = load(spec_h, spec, in_sem.at[0])
    swap_cp = load(swap_h, swap, in_sem.at[10])
    sws_cp = load(sw_h, sw_s, in_sem.at[1])
    pieces = 5
    piece = half // pieces
    leg_cps = [
        load(leg_h.at[pl.ds(i * piece, piece)], leg.at[pl.ds(i * piece, piece)], leg_sem.at[i])
        for i in range(pieces)
    ]
    others = [
        load(a, b, in_sem.at[2 + i])
        for i, (a, b) in enumerate(
            [
                (sw_h, sw),
                (waves_h, waves),
                (gw_h, gw),
                (mr_h, mr),
                (mp_h, mp),
                (vm_h, vm),
                (fac_h, fac),
                (smooth_h, smooth),
            ]
        )
    ]

    sws_cp.wait()
    spec_cp.wait()
    wave = sw_s[w] * stride
    order = lax.broadcasted_iota(jnp.int32, (1, orders), 1)
    live = jnp.where(order < orders - wave, 1.0, 0.0).astype(f32)
    parity = jnp.where(order % 2 == 0, 1.0, -1.0).astype(f32)
    masked = [spec[:, r, :] * live for r in range(2)]
    for r in range(2):
        for h in range(2):
            mask_out[2 * r + h] = masked[r][:, h * kq : (h + 1) * kq]
    coeffs = jnp.concatenate(masked, axis=0)
    coeffs = jnp.concatenate([coeffs, coeffs * parity], axis=0).astype(bf16)
    for i in range(pieces):
        leg_cps[i].wait()
        field[pl.ds(i * piece, piece), :] = dot(
            leg[pl.ds(i * piece, piece), :], coeffs, ((1,), (1,))
        )

    block = bands * tiles
    swap_cp.wait()

    def swapped(parts):
        turn = jnp.concatenate([swap[i] for i in range(groups)], axis=1)
        return dot(jnp.concatenate(parts, axis=1), turn, ((1,), (0,)))

    turned = swapped(
        [field[pl.ds(a, block, stride=groups), :].astype(bf16) for a in range(groups)]
    )
    for n in range(2):
        for r in range(2):
            q = 2 * n + r
            rows32[pl.ds(n * 2 * block + r, block, stride=2), :] = turned[
                :, q * lanes : (q + 1) * lanes
            ]
    to_grid[...] = rows32[...].astype(bf16).reshape(to_grid.shape)

    pl.semaphore_wait(barrier, slots - 1 + levs - 1)

    def place(d):
        return d + (d // bands) * (3 * bands - 1 - 2 * d)

    def forward(c, d):
        pltpu.make_async_remote_copy(
            src_ref=to_grid.at[place(d), pl.ds(*cuts[c])],
            dst_ref=at_grid.at[w, pl.ds(*cuts[c])],
            send_sem=wave_send.at[0, c],
            recv_sem=wave_recv.at[0, c],
            device_id=(d, y),
            device_id_type=MESH,
        ).start()

    for c in range(len(cuts)):
        every_peer(functools.partial(forward, c))
    own = pltpu.make_async_copy(to_grid.at[place(w)], at_grid.at[w], own_sem.at[0])
    own.start()

    def across(src, dst, k):
        cps = []
        for i in (2, 1, 3):
            to = lax.rem(y + i, levs)
            cp = pltpu.make_async_remote_copy(
                src_ref=src.at[to],
                dst_ref=dst.at[y],
                send_sem=lev_send.at[k, i - 1],
                recv_sem=lev_recv.at[k, i - 1],
                device_id=(w, to),
                device_id_type=MESH,
            )
            cp.start()
            cps.append(cp)
        dst[y] = src[y]
        return cps

    first = across(mask_out, mask_in, 0)

    for cp in others:
        cp.wait()
    for i in range(half // lanes):
        gwb[pl.ds(i * lanes, lanes), :] = jnp.broadcast_to(
            gw[pl.ds(i * lanes, lanes)].reshape(1, lanes), (lanes, lanes)
        ).T
    base = 0
    for start, count in cuts:
        size = count * groups
        for i in range(bands):
            src, dst = pl.ds(i * band + start * groups, size), pl.ds(base + i * size, size)
            legc[dst, :] = leg[src, :]
            gwbc[dst, :] = gwb[src, :]
        base += bands * size
    part_j = lax.broadcasted_iota(jnp.int32, (2 * slots, slots), 0)
    held = jnp.broadcast_to(sw[...].reshape(1, slots), (2 * slots, slots))
    choose = jnp.concatenate(
        [jnp.where(part_j == held + r * slots, 1.0, 0.0) for r in range(2)], axis=1
    ).astype(bf16)
    turned = dot(waves[...], choose, ((1,), (0,)))
    trig[...] = turned.astype(bf16)
    trig_t[...] = turned.T.astype(bf16)

    factor = fac[...]
    fhigh = factor.astype(bf16)
    flow = (factor - fhigh.astype(f32)).astype(bf16)
    half_points = points // lanes
    shigh, slow = [
        jnp.concatenate([smooth[n * half_points + i] for i in range(half_points)], axis=1)
        for n in range(2)
    ]
    top = dot(fhigh, shigh, ((1,), (0,))) + dot(flow, shigh, ((1,), (0,)))
    top += dot(fhigh, slow, ((1,), (0,)))
    root = 1.0 / math.sqrt(slots)
    top = top * root
    thigh = top.astype(bf16)
    tlow = (top - thigh.astype(f32)).astype(bf16)
    row = lax.broadcasted_iota(jnp.int32, (band, tiles * lanes), 0)
    south = w // bands
    row = row + south * (band - 1 - 2 * row)
    col = lax.broadcasted_iota(jnp.int32, (band, tiles * lanes), 1) // vl
    spread = jnp.where(row == col, 1.0, 0.0).astype(bf16)
    fbig[...] = dot(thigh, spread, ((0,), (0,))) + dot(tlow, spread, ((0,), (0,)))

    total = (wave + (y % 2) * kq + lax.broadcasted_iota(jnp.int32, (1, kq), 1)).astype(f32)
    damping = total * (total + 1.0) / float(orders * orders)
    rates = jnp.broadcast_to(mr[...].reshape(1, lanes), (lanes, lanes)).T[:, :1]
    damp[...] = 1.0 / (1.0 + rates * damping)

    def solve(x):
        modes = dot(mp[...], x, ((1,), (0,)), HIGHEST) * damp[...]
        return dot(vm[...], modes, ((1,), (0,)), HIGHEST)

    def split(x):
        high = x.astype(bf16)
        return high, (x - high.astype(f32)).astype(bf16)

    ends = [split(ref[...]) for ref in (mp, vm)]
    for k in range(2):
        pair[k] = jnp.concatenate(ends[k], axis=1)

    def solve_change(x, damping):
        modes = dot(pair[0], jnp.concatenate([x, x], axis=0), ((1,), (0,))) * damping
        high, low = split(modes)
        out = dot(pair[1], jnp.concatenate([high, high], axis=0), ((1,), (0,)))
        return out + dot(pair[1, :, :lanes], low, ((1,), (0,)))

    for cp in first:
        cp.wait()
    still_out[...] = solve(mask_in[...].reshape(levs * vl, kq)).reshape(levs, vl, kq)
    second = across(still_out, still_in, 1)

    def await_all(buf, sems, c):
        ref = buf.at[pl.ds(0, slots - 1), pl.ds(*cuts[c])]
        pltpu.make_async_copy(ref, ref, sems.at[c]).wait()

    def backward(c, d):
        pltpu.make_async_remote_copy(
            src_ref=to_slot.at[d, pl.ds(*cuts[c])],
            dst_ref=at_slot.at[place(w), pl.ds(*cuts[c])],
            send_sem=wave_send.at[1, c],
            recv_sem=wave_recv.at[1, c],
            device_id=(d, y),
            device_id_type=MESH,
        ).start()

    own.wait()
    for c, (start, count) in enumerate(cuts):
        await_all(at_grid, wave_recv.at[0], c)
        chunk = 2 * count
        here = pl.ds(0, slots * chunk)
        rows32[here, :] = (
            at_grid[:, start : start + count].reshape(slots * chunk, lanes).astype(f32)
        )
        parts = jnp.concatenate(
            [
                jnp.concatenate(
                    [rows32[pl.ds(2 * u + r, slots, stride=chunk), :] for r in range(2)], axis=0
                ).astype(bf16)
                for u in range(count)
            ],
            axis=1,
        )
        grid = dot(trig[...], parts, ((1,), (0,)))
        scaled = fbig[:, start * lanes : (start + count) * lanes]
        product = (grid * (scaled + (square_weight * root * root) * grid)).astype(bf16)
        back = dot(trig_t[...], product, ((1,), (0,)))
        back = back * ((nlon // points) / math.sqrt(nlon))
        for u in range(count):
            for r in range(2):
                field[pl.ds(2 * u + r, slots, stride=chunk), :] = back[
                    r * slots : (r + 1) * slots, u * lanes : (u + 1) * lanes
                ]
        to_slot[:, start : start + count] = (
            field[here, :].astype(bf16).reshape(slots, count, 2, lanes)
        )
        every_peer(functools.partial(backward, c))
    own = pltpu.make_async_copy(to_slot.at[w], at_slot.at[place(w)], own_sem.at[1])
    own.start()
    own.wait()
    third = []
    base = 0
    for c, (start, count) in enumerate(cuts):
        await_all(at_slot, wave_recv.at[1], c)
        size = bands * count * groups
        some = bands * count
        rows32[pl.ds(0, slots * 2 * count), :] = (
            at_slot[:, start : start + count].reshape(slots * 2 * count, lanes).astype(f32)
        )
        turned = swapped(
            [
                rows32[pl.ds(n * 2 * some + r, some, stride=2), :].astype(bf16)
                for n in range(2)
                for r in range(2)
            ]
        )
        for a in range(groups):
            field[pl.ds(a, some, stride=groups), :] = turned[:, a * lanes : (a + 1) * lanes]
        weighted = (field[pl.ds(0, size), :] * gwbc[pl.ds(base, size), :]).T.astype(bf16)
        table = legc[pl.ds(base, size), :]
        base += size
        if c < len(cuts) - 1:
            sums = dot(weighted, table, ((1,), (0,)))
            partial[...] = sums if c == 0 else partial[...] + sums
            continue
        for p, (first, width) in enumerate(splits):
            cols = [slice(h * kq + first, h * kq + first + width) for h in range(2)]
            sums = dot(
                weighted, jnp.concatenate([table[:, q] for q in cols], axis=1), ((1,), (0,))
            )
            for h in range(2):
                mine = sums[:, h * width : (h + 1) * width]
                if c:
                    mine = mine + partial[:, cols[h]]
                tend = mine[: 2 * vl] + parity[:, cols[h]] * mine[2 * vl :]
                tend = (tend * (live[:, cols[h]] * time_step)).astype(bf16)
                for r in range(2):
                    tend_out[2 * r + h, :, first : first + width] = tend[r * vl : (r + 1) * vl]
            third.append(across(tend_out, tend_in, 2 + p))
    fourth = []
    for p, (start, count) in enumerate(splits):
        for cp in third[p]:
            cp.wait()
        change = tend_in[:, :, start : start + count].reshape(levs * vl, count)
        change = solve_change(change, damp[:, start : start + count])
        move_out[:, :, start : start + count] = change.reshape(levs, vl, count).astype(bf16)
        fourth.append(across(move_out, move_in, 2 + len(splits) + p))
    for cp in second:
        cp.wait()
    for p, (start, count) in enumerate(splits):
        for cp in fourth[p]:
            cp.wait()
        for r in range(2):
            for h in range(2):
                out_ref[:, r, h * kq + start : h * kq + start + count] = still_in[
                    2 * r + h, :, start : start + count
                ] + move_in[2 * r + h, :, start : start + count].astype(f32)
    for k, buf in ((0, to_grid), (1, to_slot)):
        for c in range(len(cuts)):
            await_all(buf, wave_send.at[k], c)


def local(
    spectral,
    legendre,
    gauss_weight,
    slot_waves,
    grid_factor,
    mode_projector,
    vertical_modes,
    mode_rates,
):
    _, vl, _, orders = spectral.shape
    half = legendre.shape[1]
    band, nlon = grid_factor.shape
    slots = slot_waves.shape[0]
    nmodes = mode_rates.shape[0]
    levs = nmodes // vl
    stride = ((orders - 1) // (slots - 1) - 1) // 2 * 2 + 1
    smooth, waves = tables(slots, nlon, stride)
    points = waves.shape[0]
    kq = orders // 2
    lanes = 128
    groups = lanes // vl
    tiles = band // groups
    first = tiles // 2
    cuts = ((0, first), (first, tiles - first))
    splits = ((0, kq),)
    cfg = (slots, levs, half, orders, nlon, band, stride, cuts, splits)
    swap = swap_blocks(groups, vl)
    vmem = pltpu.VMEM
    dma = pltpu.SemaphoreType.DMA
    cells = vmem((slots, tiles, 2, lanes), bf16)
    scratch = [
        vmem((vl, 2, orders), f32),
        vmem((half, orders), bf16),
        vmem((half,), f32),
        vmem((slots,), jnp.int32),
        pltpu.SMEM((slots,), jnp.int32),
        vmem((band, nlon), f32),
        vmem((nmodes, nmodes), f32),
        vmem((nmodes, nmodes), f32),
        vmem((nmodes,), f32),
        vmem(smooth.shape, bf16),
        vmem(waves.shape, bf16),
        vmem(swap.shape, bf16),
        dma((11,)),
        dma((5,)),
        dma((2,)),
        vmem((levs, vl, kq), f32),
        vmem((levs, vl, kq), f32),
        vmem((levs, vl, kq), f32),
        vmem((levs, vl, kq), f32),
        vmem((levs, vl, kq), bf16),
        vmem((levs, vl, kq), bf16),
        vmem((levs, vl, kq), bf16),
        vmem((levs, vl, kq), bf16),
        cells,
        cells,
        cells,
        cells,
        vmem((half, lanes), f32),
        vmem((half, lanes), f32),
        vmem((half, lanes), f32),
        vmem((half, lanes), f32),
        vmem((half, orders), bf16),
        vmem((4 * vl, orders), f32),
        vmem((nmodes, kq), f32),
        vmem((points, tiles * lanes), f32),
        vmem((points, 2 * slots), bf16),
        vmem((2 * slots, points), bf16),
        vmem((2, nmodes, 2 * nmodes), bf16),
        dma((2 + 2 * len(splits), levs - 1)),
        dma((2 + 2 * len(splits), levs - 1)),
        dma((2, len(cuts))),
        dma((2, len(cuts))),
    ]
    out = pl.pallas_call(
        functools.partial(kernel, cfg),
        out_shape=pltpu.VMEM((vl, 2, orders), f32),
        in_specs=[pl.BlockSpec(memory_space=pl.ANY)] * 11,
        out_specs=pl.BlockSpec(memory_space=vmem),
        scratch_shapes=scratch,
        compiler_params=pltpu.CompilerParams(
            collective_id=0, has_side_effects=True, vmem_limit_bytes=56 * 2**20
        ),
        name="round_trip",
    )(
        spectral[0],
        legendre[0],
        gauss_weight,
        slot_waves,
        grid_factor,
        mode_projector,
        vertical_modes,
        mode_rates,
        jnp.asarray(smooth),
        jnp.asarray(waves),
        jnp.asarray(swap),
    )
    return out[None]


def solution(mesh):
    in_specs = (
        P("wave", "lev", None, None),
        P("wave", None, None),
        P(),
        P(),
        P("wave", None),
        P(),
        P(),
        P(),
    )
    out_specs = P("wave", "lev", None, None)
    return jax.shard_map(local, mesh=mesh, in_specs=in_specs, out_specs=out_specs, check_vma=False)
```
